256 devices in a mesh: row: 16 (over x, y), col: 16 (over z, core).
Axes of the slice: x: 4, y: 4, z: 8, core: 2. Of those that a mesh axis runs over, the one named last changes fastest.
Arguments:
- right_side: float32 [768, 32768], P('col', 'row'), may hold values from -6 to 6
- factor: float32 [32768, 2, 2048], P('row', None, 'col'), as said below
Outputs:
- result: float32 [768, 32768], P('col', 'row')
The draws below stay inside these ranges and needn't reach their ends.
Inputs may be any that keep to these rules, and one draw needn't show every extreme that they name: factor[slab q, q, :] is lower-triangular with its diagonal between 0.5 and 1.5; factor[slab 0, 1, :] is zero; all other entries are the factor's off-diagonal blocks.
All inputs are finite; a program needn't handle non-finite values.
Results may differ from the reference program's by a relative error of at most 0.00011.
Values sent between devices are 32-bit elements; how exact they have to be, the bound alone decides.
A program may use at most 64 MiB of HBM per device.

```python
import math
import jax
import jax.numpy as jnp
from jax import lax

NB = 2048
NRHS = 768
ROWS = 32768


def draw_factor(key, part):
    key = jax.random.fold_in(key, 7)
    key_base, key_diagonal = jax.random.split(key)
    base = jnp.clip(jax.random.normal(key_base, (ROWS, 2, NB), jnp.float32), -6.0, 6.0)
    diagonal_part = jax.random.uniform(key_diagonal, (ROWS, 2, 1), jnp.float32, 0.5, 1.5)
    row_ids = jnp.arange(ROWS, dtype=jnp.int32)[:, None, None]
    slab_ids = row_ids // NB
    local_ids = row_ids % NB
    panel_ids = jnp.arange(2, dtype=jnp.int32)[None, :, None]
    column_ids = jnp.arange(NB, dtype=jnp.int32)[None, None, :]
    scaled = base * (1.0 / math.sqrt(NB))
    inside = jnp.where(column_ids < local_ids, scaled, jnp.where(column_ids == local_ids, diagonal_part, 0.0))
    return jnp.where(slab_ids > panel_ids, scaled, jnp.where(slab_ids == panel_ids, inside, 0.0))


def steps_of(key, shape, pieces, smallest, high):
    def one(axis_at, shards_of):
        steps = jax.random.uniform(jax.random.fold_in(jax.random.fold_in(key, 6), axis_at), (shards_of,), jnp.float32, smallest / len(pieces), high / len(pieces))
        return jnp.repeat(jnp.exp(steps), shape[axis_at] // shards_of).reshape((-1,) + (1,) * (len(shape) - axis_at - 1))

    gain = one(*pieces[0])
    for cut in pieces[1:]:
        gain = gain * one(*cut)
    return gain


def bell_draw(rng, shape, spread, reach, cuts=(), kind=jnp.bfloat16):
    level = steps_of(rng, shape, cuts, -0.22, 0.18) if cuts else 1.0
    values = jax.random.normal(rng, shape, jnp.float32) * spread * level
    return jnp.minimum(jnp.maximum(values, -reach), reach).astype(kind)


def setup_inputs(seed: int = 0) -> dict:
    streams_of = jax.random.split(jax.random.key(seed), 3)
    right_side = bell_draw(streams_of[0], (NRHS, ROWS), 1.0, 6.0, ((0, 16), (1, 16)), jnp.float32)
    factor = draw_factor(jax.random.fold_in(streams_of[2], 71), 0)
    return {"right_side": right_side, "factor": factor}


def product_t(left, right):
    return lax.dot_general(left, right, (((1,), (1,)), ((), ())), precision=lax.Precision.HIGHEST, preferred_element_type=jnp.float32)


def reference(right_side, factor):
    solved_first = product_t(right_side[:, 0:NB], factor[0:NB, 0, :])
    updated = right_side[:, NB:] - product_t(solved_first, factor[NB:, 0, :])
    solved_second = product_t(updated[:, 0:NB], factor[NB:2 * NB, 1, :])
    trailing = updated[:, NB:] - product_t(solved_second, factor[2 * NB:, 1, :])
    return jnp.concatenate([solved_first, solved_second, trailing], axis=1)
```

```python
import jax
import jax.numpy as jnp
from jax import lax
from jax.experimental import pallas as pl
from jax.experimental.pallas import tpu as pltpu
from jax.sharding import PartitionSpec as P

MESH = pl.DeviceIdType.MESH
F32, BF16 = jnp.float32, jnp.bfloat16
NR = 16
NZ = 8
NB = 2048
MB = 48
KB = 128
SUB = 2
HALF = NB // 2
PIECE = HALF // SUB


def split(x):
    hi = x.astype(BF16)
    return hi, (x - hi.astype(F32)).astype(BF16)


def dot_nt(a, b):
    return lax.dot_general(a, b, (((1,), (1,)), ((), ())), preferred_element_type=F32)


def remote(src, dst, ssem, rsem, dev):
    return pltpu.make_async_remote_copy(
        src_ref=src, dst_ref=dst, send_sem=ssem, recv_sem=rsem, device_id=dev, device_id_type=MESH
    )


def loop(lo, hi, body):
    def step(i, carry):
        body(i)
        return carry

    lax.fori_loop(lo, hi, step, 0)


def kernel(
    rhs_hbm, fac_hbm, out_ref,
    fac, rhs, own, other, lhi, llo, w, wb, xs, r1, xb, t, tb, acc, slots,
    loc_sem, s_sc, r_sc, s_z, r_z, s_cx, r_cx, s_ag, r_ag, s_a, r_a, s_l, r_l, s_rs, r_rs,
):
    r = lax.axis_index("row")
    c = lax.axis_index("col")
    z = c // 2
    core = c % 2
    mate = (r, c + 1 - 2 * core)

    def rowpeer(d):
        return (r + d) % NR

    def zpeer(d):
        return (z + d) % NZ

    fac_in = pltpu.make_async_copy(fac_hbm, fac, loc_sem.at[0])
    rhs_in = pltpu.make_async_copy(rhs_hbm, rhs, loc_sem.at[1])
    fac_in.start()
    rhs_in.start()

    barrier = pltpu.get_barrier_semaphore()

    def greet_row(d):
        pl.semaphore_signal(barrier, inc=1, device_id=(rowpeer(d), c), device_id_type=MESH)

    def greet_z(d):
        pl.semaphore_signal(barrier, inc=1, device_id=(r, 2 * zpeer(d) + core), device_id_type=MESH)

    loop(1, NR, greet_row)
    loop(1, NZ, greet_z)
    pl.semaphore_signal(barrier, inc=1, device_id=mate, device_id_type=MESH)

    rhs_in.wait()
    fac_in.wait()

    def compact(i):
        for q in range(2):
            own[q, pl.ds(pl.multiple_of(i * 256, 256), 256), :] = fac[pl.ds(i * 512 + q, 256, stride=2), :]

    loop(0, NB // 256, compact)
    pl.semaphore_wait(barrier, NR - 1 + NZ - 1 + 1)

    def cols(p):
        return pl.ds(pl.multiple_of(p * KB, KB), KB)

    def sc_rhs(panel, p):
        dst = xs.at[0, p] if panel == 0 else r1
        return remote(rhs.at[:, cols(p)], dst, s_sc.at[0, p], r_sc.at[0 if panel == 0 else 1], (p, c))

    def sc_fac(which, p):
        return remote(own.at[which // 2, cols(p)], w.at[which, c], s_sc.at[1 + which // 2, p], r_sc.at[2 + which], (p, c))

    @pl.when(r == 0)
    def _():
        loop(1, NR, lambda d: sc_rhs(0, rowpeer(d)).start())
        loop(1, NR, lambda d: sc_fac(0, rowpeer(d)).start())
        xs[0, 0] = rhs[:, 0:KB]
        w[0, c] = own[0, 0:KB, :]

    @pl.when(r == 1)
    def _():
        loop(1, NR, lambda d: sc_fac(1, rowpeer(d)).start())
        loop(1, NR, lambda d: sc_rhs(1, rowpeer(d)).start())
        loop(1, NR, lambda d: sc_fac(2, rowpeer(d)).start())
        r1[...] = rhs[:, KB : 2 * KB]
        w[1, c] = own[0, KB : 2 * KB, :]
        w[2, c] = own[1, KB : 2 * KB, :]

    def swap(q):
        return remote(own.at[q], other.at[q], s_l.at[q], r_l.at[q], mate)

    for q in range(2):
        swap(q).start()

    def convert(src, lane):
        def step(i):
            at = pl.ds(pl.multiple_of(i * 256, 256), 256)
            for q in range(2):
                hi, lo = split(src[q, at, :])
                lhi[q, at, pl.ds(pl.multiple_of(lane * KB, KB), KB)] = hi
                llo[q, at, pl.ds(pl.multiple_of(lane * KB, KB), KB)] = lo

        loop(0, NB // 256, step)

    convert(own, core)

    def ag(b, d):
        return remote(xs.at[b, r], xs.at[b, r], s_ag.at[b, d], r_ag.at[b, r], (rowpeer(d), c))

    def ag_in(b, d):
        p = rowpeer(d)
        return remote(xs.at[b, p], xs.at[b, p], s_ag.at[b, d], r_ag.at[b, p], (p, c))

    def ag_start(b):
        loop(1, NR, lambda d: ag(b, d).start())

    def ag_wait(b):
        loop(1, NR, lambda d: ag_in(b, d).wait_recv())

    def zsend(q, d):
        return remote(w.at[q, c], w.at[q, c], s_z.at[q, d], r_z.at[q, z], (r, 2 * zpeer(d) + core))

    def zrecv(q, d):
        k = 2 * zpeer(d) + core
        return remote(w.at[q, k], w.at[q, k], s_z.at[q, d], r_z.at[q, zpeer(d)], (r, k))

    def xsend(q, d):
        k = 2 * zpeer(d) + core
        return remote(w.at[q, k], w.at[q, k], s_cx.at[q, d], r_cx.at[q, zpeer(d)], mate)

    def xrecv(q, d):
        k = 2 * zpeer(d) + 1 - core
        return remote(w.at[q, k], w.at[q, k], s_cx.at[q, d], r_cx.at[q, zpeer(d)], mate)

    def ready(q, k):
        hi, lo = split(w[q, k])
        at = cols(k)
        wb[q, 0:KB, at] = hi
        wb[q, KB : 2 * KB, at] = lo

    def fetch(q):
        @pl.when(r != q - q // 2)
        def _():
            remote(w.at[q, c], w.at[q, c], s_sc.at[1, 0], r_sc.at[2 + q], (rowpeer(1), c)).wait_recv()

        loop(1, NZ, lambda d: zsend(q, d).start())
        xsend(q, 0).start()
        ready(q, c)

    def forward(q, lo, hi):
        def step(i):
            h = (i + 2) // 2
            d = h + i % 2 * (NZ - 2 * h)
            zrecv(q, d).wait_recv()
            xsend(q, d).start()
            ready(q, 2 * zpeer(d) + core)

        loop(lo, hi, step)

    def collect(q):
        def step(d):
            xrecv(q, d).wait_recv()
            ready(q, 2 * zpeer(d) + 1 - core)

        loop(0, NZ, step)

    def load_x(b):
        def step(k):
            hi, lo = split(xs[b, k])
            xb[0:MB, cols(k)] = hi
            xb[MB : 2 * MB, cols(k)] = lo

        loop(0, NR, step)

    def product(q):
        o = dot_nt(xb[...], wb[q])
        return o[0:MB, 0:KB] + o[MB : 2 * MB, 0:KB] + o[0:MB, KB : 2 * KB]

    @pl.when(r != 0)
    def _():
        remote(xs.at[0, r], xs.at[0, r], s_sc.at[0, 0], r_sc.at[0], (rowpeer(1), c)).wait_recv()

    ag_start(0)
    fetch(0)
    for q in range(2):
        swap(q).wait_recv()
    convert(other, 1 - core)
    ag_wait(0)
    load_x(0)
    forward(0, 0, 5)
    fetch(1)
    forward(0, 5, 7)
    collect(0)
    xs[1, r] = product(0)
    ag_start(1)
    forward(1, 0, 5)
    fetch(2)
    forward(1, 5, 7)
    collect(1)
    ag_wait(1)
    load_x(1)

    @pl.when(r != 1)
    def _():
        remote(r1, r1, s_sc.at[0, 0], r_sc.at[1], (rowpeer(1), c)).wait_recv()

    xs[2, r] = r1[...] - product(1)
    ag_start(2)

    def a2a(q, d):
        p = zpeer(d)
        return remote(xs.at[1 + 2 * q, pl.ds(2 * p, 2)], t.at[q, z], s_a.at[q, d], r_a.at[q, z], (r, 2 * p + core))

    def a2a_in(q, d):
        p = zpeer(d)
        return remote(t.at[q, p], t.at[q, p], s_a.at[q, d], r_a.at[q, p], (r, 2 * p + core))

    def regroup_start(q):
        loop(1, NZ, lambda d: a2a(q, d).start())
        t[q, z] = xs[1 + 2 * q, pl.ds(2 * z, 2)]

    def regroup_wait(q):
        loop(1, NZ, lambda d: a2a_in(q, d).wait_recv())

    def load_t(q):
        def step(d):
            for k in range(2):
                hi, lo = split(t[q, d, k])
                tb[0, pl.ds(pl.multiple_of(d * MB, MB), MB), k * KB : (k + 1) * KB] = hi
                tb[1, pl.ds(pl.multiple_of(d * MB, MB), MB), k * KB : (k + 1) * KB] = lo

        loop(0, NZ, step)

    regroup_start(0)
    forward(2, 0, 7)
    collect(2)
    ag_wait(2)
    load_x(2)
    xs[3, r] = product(2)
    ag_start(3)
    regroup_wait(0)
    load_t(0)

    def first_part(i):
        at = pl.ds(pl.multiple_of(i * 256, 256), 256)
        hi, lo = tb[0], tb[1]
        o = dot_nt(hi, lhi[0, at, :]) + dot_nt(lo, lhi[0, at, :]) + dot_nt(hi, llo[0, at, :])
        acc[:, :, at] = o.reshape(NZ, MB, 256)

    loop(0, NB // 256, first_part)
    ag_wait(3)
    regroup_start(1)
    regroup_wait(1)
    load_t(1)

    def dest(way, s):
        return (z + NZ - 1 - s) % NZ if way == 0 else (z + 1 + s) % NZ

    def second_part(s):
        for way in range(2):
            d = dest(way, s)
            rows = pl.ds(pl.multiple_of(d * MB, MB), MB)
            hi, lo = tb[0, rows, :], tb[1, rows, :]
            both = jnp.concatenate([hi, lo], axis=0)
            for j in range(HALF // 512):
                at = slice(way * HALF + j * 512, way * HALF + (j + 1) * 512)
                o = dot_nt(both, lhi[1, at, :])
                acc[d, :, at] += o[0:MB] + o[MB : 2 * MB] + dot_nt(hi, llo[1, at, :])

    def hop(way, s, j):
        lanes = pl.ds(way * HALF + j * PIECE, PIECE)
        to = (z + 1) % NZ if way == 0 else (z + NZ - 1) % NZ
        return remote(
            acc.at[dest(way, s), :, lanes], slots.at[way, s, j], s_rs.at[way, s, j], r_rs.at[way, s, j],
            (r, 2 * to + core),
        )

    def take(s):
        for j in range(SUB):
            for way in range(2):
                lanes = slice(way * HALF + j * PIECE, way * HALF + (j + 1) * PIECE)
                hop(way, s, j).wait_recv()
                acc[dest(way, s + 1), :, lanes] += slots[way, s, j]
                yield_send(way, s + 1, j)

    def yield_send(way, s, j):
        @pl.when(s < NZ - 1)
        def _():
            hop(way, s, j).start()

    second_part(0)
    for j in range(SUB):
        for way in range(2):
            hop(way, 0, j).start()

    def ring(s):
        second_part(s + 1)
        take(s)

    loop(0, NZ - 1, ring)

    @pl.when(r == 0)
    def _():
        for k in range(NR):
            out_ref[:, k * KB : (k + 1) * KB] = xs[1, k]

    @pl.when(r == 1)
    def _():
        for k in range(NR):
            out_ref[:, k * KB : (k + 1) * KB] = xs[3, k]

    @pl.when(r > 1)
    def _():
        out_ref[...] = rhs[...] - acc[z]

    @pl.when(r == 0)
    def _():
        loop(1, NR, lambda d: sc_rhs(0, rowpeer(d)).wait_send())
        loop(1, NR, lambda d: sc_fac(0, rowpeer(d)).wait_send())

    @pl.when(r == 1)
    def _():
        loop(1, NR, lambda d: sc_fac(1, rowpeer(d)).wait_send())
        loop(1, NR, lambda d: sc_rhs(1, rowpeer(d)).wait_send())
        loop(1, NR, lambda d: sc_fac(2, rowpeer(d)).wait_send())

    for q in range(2):
        swap(q).wait_send()
        loop(1, NZ, lambda d, q=q: a2a(q, d).wait_send())
    for q in range(3):
        loop(1, NZ, lambda d, q=q: zsend(q, d).wait_send())
        loop(0, NZ, lambda d, q=q: xsend(q, d).wait_send())
    for b in range(4):
        loop(1, NR, lambda d, b=b: ag(b, d).wait_send())

    def drain(s):
        for way in range(2):
            for j in range(SUB):
                hop(way, s, j).wait_send()

    loop(0, NZ - 1, drain)


def local(right_side, factor):
    rows = factor.shape[0]
    dma = pltpu.SemaphoreType.DMA
    return pl.pallas_call(
        kernel,
        name="panels",
        out_shape=jax.ShapeDtypeStruct((MB, NB), F32),
        in_specs=[pl.BlockSpec(memory_space=pl.ANY)] * 2,
        out_specs=pl.BlockSpec(memory_space=pltpu.VMEM),
        scratch_shapes=[
            pltpu.VMEM((2 * NB, KB), F32),
            pltpu.VMEM((MB, NB), F32),
            pltpu.VMEM((2, NB, KB), F32),
            pltpu.VMEM((2, NB, KB), F32),
            pltpu.VMEM((2, NB, 2 * KB), BF16),
            pltpu.VMEM((2, NB, 2 * KB), BF16),
            pltpu.VMEM((3, 16, KB, KB), F32),
            pltpu.VMEM((3, 2 * KB, NB), BF16),
            pltpu.VMEM((4, NR, MB, KB), F32),
            pltpu.VMEM((MB, KB), F32),
            pltpu.VMEM((2 * MB, NB), BF16),
            pltpu.VMEM((2, NZ, 2, MB, KB), F32),
            pltpu.VMEM((2, NZ * MB, 2 * KB), BF16),
            pltpu.VMEM((NZ, MB, NB), F32),
            pltpu.VMEM((2, NZ - 1, SUB, MB, PIECE), F32),
            dma((2,)),
            dma((3, NR)),
            dma((5,)),
            dma((3, NZ)),
            dma((3, NZ)),
            dma((3, NZ)),
            dma((3, NZ)),
            dma((4, NR)),
            dma((4, NR)),
            dma((2, NZ)),
            dma((2, NZ)),
            dma((2,)),
            dma((2,)),
            dma((2, NZ - 1, SUB)),
            dma((2, NZ - 1, SUB)),
        ],
        compiler_params=pltpu.CompilerParams(
            collective_id=0, has_side_effects=True, vmem_limit_bytes=50 * 2**20
        ),
    )(right_side, factor.reshape(2 * rows, KB))


def solution(mesh):
    in_specs = (P("col", "row"), P("row", None, "col"))
    out_specs = P("col", "row")
    return jax.shard_map(local, mesh=mesh, in_specs=in_specs, out_specs=out_specs, check_vma=False)
```

```python
import jax
import jax.numpy as jnp
from jax import lax
from jax.experimental import pallas as pl
from jax.experimental.pallas import tpu as pltpu
from jax.sharding import PartitionSpec as P

STOP = 99
MESH = pl.DeviceIdType.MESH
F32, BF16 = jnp.float32, jnp.bfloat16
NR = 16
NX = 4
NZ = 8
NB = 2048
MB = 48
KB = 128
MC = NZ * MB
SUB = 2
HALF = NB // 2
PIECE = HALF // SUB


def split(x):
    hi = x.astype(BF16)
    return hi, (x - hi.astype(F32)).astype(BF16)


def dot_nt(a, b):
    return lax.dot_general(a, b, (((1,), (1,)), ((), ())), preferred_element_type=F32)


def remote(src, dst, ssem, rsem, dev):
    return pltpu.make_async_remote_copy(
        src_ref=src, dst_ref=dst, send_sem=ssem, recv_sem=rsem, device_id=dev, device_id_type=MESH
    )


def loop(lo, hi, body):
    def step(i, carry):
        body(i)
        return carry

    lax.fori_loop(lo, hi, step, 0)


def kernel(
    rhs_hbm, fac_hbm, out_ref,
    fac, rhs, own, other, lhi, llo, w, rel, wb, xs, r1, xb, t, py, pz, gx, s1t, tb, acc, slots,
    loc_sem, s_rhs, r_rhs, s_sc, r_sc, s_rel, r_rel, s_z, r_z, s_cx, r_cx, s_ag, r_ag, s_a, r_a, s_g, r_g, s_o, r_o,
    s_l, r_l, s_rs, r_rs,
):
    r = lax.axis_index("row")
    c = lax.axis_index("col")
    z = c // 2
    core = c % 2
    mate = (r, c + 1 - 2 * core)

    def rowpeer(d):
        return (r + d) % NR

    def zpeer(d):
        return (z + d) % NZ

    fac_in = pltpu.make_async_copy(fac_hbm, fac, loc_sem.at[0])
    rhs_in = pltpu.make_async_copy(rhs_hbm, rhs, loc_sem.at[1])
    fac_in.start()
    rhs_in.start()

    barrier = pltpu.get_barrier_semaphore()

    def greet_row(d):
        pl.semaphore_signal(barrier, inc=1, device_id=(rowpeer(d), c), device_id_type=MESH)

    def greet_z(d):
        pl.semaphore_signal(barrier, inc=1, device_id=(r, 2 * zpeer(d) + core), device_id_type=MESH)

    loop(1, NR, greet_row)
    loop(1, NZ, greet_z)
    pl.semaphore_signal(barrier, inc=1, device_id=mate, device_id_type=MESH)

    rhs_in.wait()
    fac_in.wait()

    def compact(i):
        for q in range(2):
            own[q, i] = fac[pl.ds(i * 512 + q, 256, stride=2), :].reshape(16, 16, KB)

    loop(0, NZ, compact)
    py[...] = jnp.zeros_like(py)
    pl.semaphore_wait(barrier, NR - 1 + NZ - 1 + 1)

    def cols(p):
        return pl.ds(pl.multiple_of(p * KB, KB), KB)

    def slice_of(which, p, h):
        if which == 2:
            return own.at[1, pl.ds(4 * h, 4), p]
        return own.at[0, p // 2, pl.ds(p % 2 * 8 + 4 * h, 4)]

    def half(q, k, h):
        return w.at[q, k, pl.ds(4 * h, 4)]

    def sc_rhs(panel, p):
        dst = xs.at[0, p] if panel == 0 else r1
        return remote(rhs.at[:, cols(p)], dst, s_rhs.at[p], r_rhs.at[panel], (p, c))

    def source(which):
        return 0 if which == 0 else 1

    def far(which, p):
        return jnp.logical_and(p // NX == 2, p % NX != source(which))

    def sc_fac(which, p, h):
        return remote(slice_of(which, p, h), half(which, c, h), s_sc.at[which, h, p], r_sc.at[which, h], (p, c))

    def sc_far(which, p, h):
        to = rel.at[which, pl.ds(4 * h, 4)]
        return remote(slice_of(which, p, h), to, s_sc.at[which, h, p], r_rel.at[which, h], (p % NX, c))

    def relay(which, h):
        got = rel.at[which, pl.ds(4 * h, 4)]
        return remote(got, half(which, c, h), s_rel.at[which, h], r_sc.at[which, h], ((r + 2 * NX) % NR, c))

    def sc_fac_go(which, h, act):
        def step(d):
            p = rowpeer(d)
            f = far(which, p)

            @pl.when(f)
            def _():
                act(sc_far(which, p, h))

            @pl.when(jnp.logical_not(f))
            def _():
                act(sc_fac(which, p, h))

        loop(1, NR, step)

    def sc_fac_start(which):
        for h in range(2):
            sc_fac_go(which, h, lambda cp: cp.start())

    def sc_fac_left(which):
        for h in range(2):
            sc_fac_go(which, h, lambda cp: cp.wait_send())

    def is_relay(which):
        return jnp.logical_and(r < NX, r != source(which))

    def relay_go(which, h):
        @pl.when(is_relay(which))
        def _():
            got = rel.at[which, pl.ds(4 * h, 4)]
            remote(got, got, s_rel.at[which, h], r_rel.at[which, h], (rowpeer(1), c)).wait_recv()
            relay(which, h).start()

    def rhs_start(panel):
        @pl.when(r == panel)
        def _():
            loop(1, NR, lambda d: sc_rhs(panel, rowpeer(d)).start())

    def last_start():
        @pl.when(r == 1)
        def _():
            sc_fac_start(2)

    @pl.when(r == 0)
    def _():
        sc_fac_start(0)
        xs[0, 0] = rhs[:, 0:KB]
        w[0, c] = own[0, 0, 0:8]

    @pl.when(r == 1)
    def _():
        sc_fac_start(1)
        r1[...] = rhs[:, KB : 2 * KB]
        w[1, c] = own[0, 0, 8:16]
        w[2, c] = own[1, :, 1]

    def swap(q):
        return remote(own.at[q], other.at[q], s_l.at[q], r_l.at[q], mate)

    for q in range(2):
        swap(q).start()

    def convert(src, lane):
        def step(i):
            at = pl.ds(pl.multiple_of(i * 256, 256), 256)
            for q in range(2):
                hi, lo = split(src[q, i].reshape(256, KB))
                lhi[q, at, cols(lane)] = hi
                llo[q, at, cols(lane)] = lo

        loop(0, NZ, step)

    def ag(b, d):
        return remote(xs.at[b, r], xs.at[b, r], s_ag.at[b, d], r_ag.at[b, r], (rowpeer(d), c))

    def ag_in(b, d):
        p = rowpeer(d)
        return remote(xs.at[b, p], xs.at[b, p], s_ag.at[b, d], r_ag.at[b, p], (p, c))

    def ag_start(b):
        loop(1, NR, lambda d: ag(b, d).start())

    def ag_wait(b):
        loop(1, NR, lambda d: ag_in(b, d).wait_recv())

    def zcopy(q, h, i, far_z, d):
        k = 2 * far_z + core
        return remote(half(q, k, h), half(q, k, h), s_z.at[q, h, i], r_z.at[q, h, far_z], (r, 2 * zpeer(d) + core))

    def zfirst(q, h):
        return [zcopy(q, h, i, z, d) for i, d in enumerate((2, NZ - 2, 1, NZ - 1))]

    def zsecond(q, h):
        left, right = zpeer(NZ - 2), zpeer(2)
        last = zcopy(q, h, 6, left, 2) if h == 0 else zcopy(q, h, 6, right, NZ - 2)
        return [last, zcopy(q, h, 4, left, 1), zcopy(q, h, 5, right, NZ - 1)]

    def zin(q, h, d):
        zcopy(q, h, 0, zpeer(d), 1).wait_recv()

    def xsend(q, d):
        k = 2 * zpeer(d) + core
        return remote(w.at[q, k], w.at[q, k], s_cx.at[q, d], r_cx.at[q, zpeer(d)], mate)

    def xrecv(q, d):
        k = 2 * zpeer(d) + 1 - core
        return remote(w.at[q, k], w.at[q, k], s_cx.at[q, d], r_cx.at[q, zpeer(d)], mate)

    def ready(q, k):
        hi, lo = split(w[q, k].reshape(KB, KB))
        at = cols(k)
        wb[q, 0:KB, at] = hi
        wb[q, KB : 2 * KB, at] = lo

    def slice_in(q, h):
        @pl.when(r != source(q))
        def _():
            remote(half(q, c, h), half(q, c, h), s_rhs.at[0], r_sc.at[q, h], (rowpeer(1), c)).wait_recv()

    def fetch(q):
        for h in range(2):
            relay_go(q, h)
            slice_in(q, h)
            for cp in zfirst(q, h):
                cp.start()
        xsend(q, 0).start()
        ready(q, c)

    def hand_on(q, h):
        zin(q, h, 2)
        zin(q, h, NZ - 2)
        for cp in zsecond(q, h):
            cp.start()

    def near(q):
        for d in (2, NZ - 2):
            xsend(q, d).start()
            ready(q, 2 * zpeer(d) + core)
        arrive(q, (1, NZ - 1))

    def arrive(q, which):
        for d in which:
            for h in range(2):
                zin(q, h, d)
            xsend(q, d).start()
            ready(q, 2 * zpeer(d) + core)

    def collect(q):
        def step(d):
            xrecv(q, d).wait_recv()
            ready(q, 2 * zpeer(d) + 1 - core)

        loop(0, NZ, step)

    def load_x(b):
        def step(k):
            hi, lo = split(xs[b, k])
            xb[0:MB, cols(k)] = hi
            xb[MB : 2 * MB, cols(k)] = lo

        loop(0, NR, step)

    def product(q):
        o = dot_nt(xb[...], wb[q])
        return o[0:MB, 0:KB] + o[MB : 2 * MB, 0:KB] + o[0:MB, KB : 2 * KB]

    def rhs0_in():
        @pl.when(r != 0)
        def _():
            remote(xs.at[0, r], xs.at[0, r], s_rhs.at[0], r_rhs.at[0], (rowpeer(1), c)).wait_recv()

    def rhs1_in():
        @pl.when(r != 1)
        def _():
            remote(r1, r1, s_rhs.at[0], r_rhs.at[1], (rowpeer(1), c)).wait_recv()

    def swap_in():
        for q in range(2):
            swap(q).wait_recv()

    def a2a(d):
        p = zpeer(d)
        return remote(xs.at[1, pl.ds(2 * p, 2)], t.at[z], s_a.at[0, d], r_a.at[0, z], (r, 2 * p + core))

    def a2a_in(d):
        p = zpeer(d)
        return remote(t.at[p], t.at[p], s_a.at[0, d], r_a.at[0, p], (r, 2 * p + core))

    def regroup(d):
        p = zpeer(d)
        return remote(py.at[p], pz.at[z], s_a.at[1, d], r_a.at[1, z], (r, 2 * p + core))

    def regroup_in(d):
        p = zpeer(d)
        return remote(pz.at[p], pz.at[p], s_a.at[1, d], r_a.at[1, p], (r, 2 * p + core))

    def spread(g, d):
        return remote(gx.at[g, r], gx.at[g, r], s_g.at[g, d], r_g.at[g, r], (rowpeer(d), c))

    def spread_in(g, d):
        p = rowpeer(d)
        return remote(gx.at[g, p], gx.at[g, p], s_g.at[g, d], r_g.at[g, p], (p, c))

    def to_owner():
        return remote(py, s1t.at[:, r], s_o, r_o.at[r], (1, c))

    def from_peer(d):
        p = rowpeer(d)
        return remote(py, s1t.at[:, p], s_o, r_o.at[p], (p, c))

    def dest(way, s):
        return (z + NZ - 1 - s) % NZ if way == 0 else (z + 1 + s) % NZ

    def hop(way, s, j):
        lanes = pl.ds(way * HALF + j * PIECE, PIECE)
        to = (z + 1) % NZ if way == 0 else (z + NZ - 1) % NZ
        return remote(
            acc.at[dest(way, s), :, lanes], slots.at[way, s, j], s_rs.at[way, s, j], r_rs.at[way, s, j],
            (r, 2 * to + core),
        )

    def left_scatter():
        @pl.when(r == 0)
        def _():
            loop(1, NR, lambda d: sc_rhs(0, rowpeer(d)).wait_send())
            sc_fac_left(0)

        @pl.when(r == 1)
        def _():
            loop(1, NR, lambda d: sc_rhs(1, rowpeer(d)).wait_send())
            sc_fac_left(1)
            sc_fac_left(2)

        for which in range(3):

            @pl.when(is_relay(which))
            def _(which=which):
                for h in range(2):
                    relay(which, h).wait_send()

    def left_swap():
        for q in range(2):
            swap(q).wait_send()

    def left_f(q):
        for h in range(2):
            for cp in zfirst(q, h) + zsecond(q, h):
                cp.wait_send()
        loop(0, NZ, lambda d: xsend(q, d).wait_send())

    def left_ag(b):
        loop(1, NR, lambda d: ag(b, d).wait_send())

    def left_a2a():
        loop(1, NZ, lambda d: a2a(d).wait_send())

    def left_regroup():
        loop(1, NZ, lambda d: regroup(d).wait_send())

    def left_spread():
        for g in range(4):
            loop(1, NR, lambda d, g=g: spread(g, d).wait_send())

    def left_ring():
        def drain(s):
            for way in range(2):
                for j in range(SUB):
                    hop(way, s, j).wait_send()

        loop(0, NZ - 1, drain)

    convert(own, core)
    fetch(0)
    rhs_start(0)
    fetch(1)
    rhs0_in()
    ag_start(0)
    hand_on(0, 0)
    hand_on(0, 1)
    last_start()
    near(0)
    hand_on(1, 0)
    hand_on(1, 1)
    arrive(0, (3, NZ - 3, 4))
    rhs_start(1)
    near(1)
    fetch(2)
    ag_wait(0)
    load_x(0)
    collect(0)
    xs[1, r] = product(0)
    ag_start(1)
    hand_on(2, 0)
    hand_on(2, 1)
    arrive(1, (3, NZ - 3, 4))
    swap_in()
    convert(other, 1 - core)
    near(2)
    arrive(2, (3, NZ - 3, 4))
    ag_wait(1)
    load_x(1)
    loop(1, NZ, lambda d: a2a(d).start())
    t[z] = xs[1, pl.ds(2 * z, 2)]
    collect(1)
    rhs1_in()
    xs[2, r] = r1[...] - product(1)
    ag_start(2)
    ag_wait(2)
    collect(2)
    load_x(2)
    turned = dot_nt(wb[2], xb[0:MB, :])
    turned = turned[0:KB] + turned[KB : 2 * KB] + dot_nt(wb[2, 0:KB, :], xb[MB : 2 * MB, :])
    py[:, :, 0:MB] = turned.reshape(NZ, 16, MB)
    loop(1, NZ, lambda d: regroup(d).start())
    pz[z] = py[z]

    @pl.when(r != 1)
    def _():
        to_owner().start()

    @pl.when(r == 1)
    def _():
        s1t[:, 1] = py[...]

    loop(1, NZ, lambda d: a2a_in(d).wait_recv())

    def load_t(d):
        for k in range(2):
            hi, lo = split(t[d, k])
            tb[0, pl.ds(pl.multiple_of(d * MB, MB), MB), k * KB : (k + 1) * KB] = hi
            tb[1, pl.ds(pl.multiple_of(d * MB, MB), MB), k * KB : (k + 1) * KB] = lo

    loop(0, NZ, load_t)

    def first_part(i):
        at = pl.ds(pl.multiple_of(i * 256, 256), 256)
        hi, lo = tb[0], tb[1]
        o = dot_nt(hi, lhi[0, at, :]) + dot_nt(lo, lhi[0, at, :]) + dot_nt(hi, llo[0, at, :])
        acc[:, :, at] = o.reshape(NZ, MB, 256)

    loop(1, NZ, lambda d: regroup_in(d).wait_recv())

    def pair(g):
        return (z + NZ - 1 - g) % NZ, z if g == 3 else (z + 1 + g) % NZ

    def spread_start(g):
        one, two = pair(g)
        gx[g, r] = pz[one] + pltpu.roll(pz[two], MB, 1)
        loop(1, NR, lambda d: spread(g, d).start())

    def spread_end(g):
        loop(1, NR, lambda d: spread_in(g, d).wait_recv())
        for k in range(2):
            hi, lo = split(gx[g, 8 * k : 8 * k + 8].reshape(KB, KB).T)
            for i, d in enumerate(pair(g)):
                rows = pl.ds(pl.multiple_of(d * MB, MB), MB)
                tb[0, rows, k * KB : (k + 1) * KB] = hi[i * MB : (i + 1) * MB]
                tb[1, rows, k * KB : (k + 1) * KB] = lo[i * MB : (i + 1) * MB]

    spread_start(0)
    loop(0, NB // 256, first_part)
    spread_end(0)

    def second_part(s):
        for way in range(2):
            d = dest(way, s)
            rows = pl.ds(pl.multiple_of(d * MB, MB), MB)
            hi, lo = tb[0, rows, :], tb[1, rows, :]
            both = jnp.concatenate([hi, lo], axis=0)
            for j in range(HALF // 512):
                at = slice(way * HALF + j * 512, way * HALF + (j + 1) * 512)
                o = dot_nt(both, lhi[1, at, :])
                acc[d, :, at] += o[0:MB] + o[MB : 2 * MB] + dot_nt(hi, llo[1, at, :])

    def pass_on(way, s, j):
        @pl.when(jnp.int32(s) < NZ - 1)
        def _():
            hop(way, s, j).start()

    def ring(s):
        if isinstance(s, int) and s < 3:
            spread_end(s + 1)
            if s < 2:
                spread_start(s + 2)
        second_part(s + 1)
        for j in range(SUB):
            for way in range(2):
                lanes = slice(way * HALF + j * PIECE, way * HALF + (j + 1) * PIECE)
                hop(way, s, j).wait_recv()
                acc[dest(way, s + 1), :, lanes] += slots[way, s, j]
                pass_on(way, s + 1, j)

    second_part(0)
    for j in range(SUB):
        for way in range(2):
            hop(way, 0, j).start()
    spread_start(1)
    for s in range(3):
        ring(s)
    loop(3, NZ - 1, ring)

    @pl.when(r == 0)
    def _():
        for k in range(NR):
            out_ref[:, k * KB : (k + 1) * KB] = xs[1, k]

    @pl.when(r == 1)
    def _():
        loop(1, NR, lambda d: from_peer(d).wait_recv())
        for k in range(NR):
            block = s1t[k // 2, k % 2 * 8 : k % 2 * 8 + 8].reshape(KB, KB)
            out_ref[:, k * KB : (k + 1) * KB] = block.T[0:MB]

    @pl.when(r > 1)
    def _():
        out_ref[...] = rhs[...] - acc[z]

    @pl.when(r != 1)
    def _():
        to_owner().wait_send()

    left_scatter()
    left_swap()
    for q in range(3):
        left_f(q)
        left_ag(q)
    left_a2a()
    left_regroup()
    left_spread()
    left_ring()


def local(right_side, factor):
    rows = factor.shape[0]
    dma = pltpu.SemaphoreType.DMA
    return pl.pallas_call(
        kernel,
        name="panels",
        out_shape=jax.ShapeDtypeStruct((MB, NB), F32),
        in_specs=[pl.BlockSpec(memory_space=pl.ANY)] * 2,
        out_specs=pl.BlockSpec(memory_space=pltpu.VMEM),
        scratch_shapes=[
            pltpu.VMEM((2 * NB, KB), F32),
            pltpu.VMEM((MB, NB), F32),
            pltpu.VMEM((2, NZ, 16, 16, KB), F32),
            pltpu.VMEM((2, NZ, 16, 16, KB), F32),
            pltpu.VMEM((2, NB, 2 * KB), BF16),
            pltpu.VMEM((2, NB, 2 * KB), BF16),
            pltpu.VMEM((3, 16, 8, 16, KB), F32),
            pltpu.VMEM((3, 8, 16, KB), F32),
            pltpu.VMEM((3, 2 * KB, NB), BF16),
            pltpu.VMEM((3, NR, MB, KB), F32),
            pltpu.VMEM((MB, KB), F32),
            pltpu.VMEM((2 * MB, NB), BF16),
            pltpu.VMEM((NZ, 2, MB, KB), F32),
            pltpu.VMEM((NZ, 16, KB), F32),
            pltpu.VMEM((NZ, 16, KB), F32),
            pltpu.VMEM((4, NR, 16, KB), F32),
            pltpu.VMEM((NZ, NR, 16, KB), F32),
            pltpu.VMEM((2, MC, 2 * KB), BF16),
            pltpu.VMEM((NZ, MB, NB), F32),
            pltpu.VMEM((2, NZ - 1, SUB, MB, PIECE), F32),
            dma((2,)),
            dma((NR,)),
            dma((2,)),
            dma((3, 2, NR)),
            dma((3, 2)),
            dma((3, 2)),
            dma((3, 2)),
            dma((3, 2, 7)),
            dma((3, 2, NZ)),
            dma((3, NZ)),
            dma((3, NZ)),
            dma((3, NR)),
            dma((3, NR)),
            dma((2, NZ)),
            dma((2, NZ)),
            dma((4, NR)),
            dma((4, NR)),
            dma,
            dma((NR,)),
            dma((2,)),
            dma((2,)),
            dma((2, NZ - 1, SUB)),
            dma((2, NZ - 1, SUB)),
        ],
        compiler_params=pltpu.CompilerParams(
            collective_id=0, has_side_effects=True, vmem_limit_bytes=60 * 2**20
        ),
    )(right_side, factor.reshape(2 * rows, KB))


def solution(mesh):
    in_specs = (P("col", "row"), P("row", None, "col"))
    out_specs = P("col", "row")
    return jax.shard_map(local, mesh=mesh, in_specs=in_specs, out_specs=out_specs, check_vma=False)
```

```python
import jax
import jax.numpy as jnp
from jax import lax
from jax.experimental import pallas as pl
from jax.experimental.pallas import tpu as pltpu
from jax.sharding import PartitionSpec as P

STOP = 99
MESH = pl.DeviceIdType.MESH
F32, BF16 = jnp.float32, jnp.bfloat16
NR = 16
NX = 4
NZ = 8
NB = 2048
MB = 48
KB = 128
MC = NZ * MB
SUB = 2
HALF = NB // 2
PIECE = HALF // SUB


def split(x):
    hi = x.astype(BF16)
    return hi, (x - hi.astype(F32)).astype(BF16)


def dot_nt(a, b):
    return lax.dot_general(a, b, (((1,), (1,)), ((), ())), preferred_element_type=F32)


def remote(src, dst, ssem, rsem, dev):
    return pltpu.make_async_remote_copy(
        src_ref=src, dst_ref=dst, send_sem=ssem, recv_sem=rsem, device_id=dev, device_id_type=MESH
    )


def loop(lo, hi, body):
    def step(i, carry):
        body(i)
        return carry

    lax.fori_loop(lo, hi, step, 0)


def kernel(
    rhs_hbm, fac_hbm, out_ref,
    fac, rhs, own, other, lhi, llo, w, rel, wb, xs, r1, xb, t, py, pz, gx, s1t, ta, tb, acc, slots,
    loc_sem, s_rhs, r_rhs, s_sc, r_sc, s_rel, r_rel, s_z, r_z, s_cx, r_cx, s_ag, r_ag, s_a, r_a, s_g, r_g, s_o, r_o,
    s_l, r_l, s_rs, r_rs,
):
    r = lax.axis_index("row")
    c = lax.axis_index("col")
    z = c // 2
    core = c % 2
    mate = (r, c + 1 - 2 * core)

    def rowpeer(d):
        return (r + d) % NR

    def zpeer(d):
        return (z + d) % NZ

    fac_in = pltpu.make_async_copy(fac_hbm, fac, loc_sem.at[0])
    rhs_in = pltpu.make_async_copy(rhs_hbm, rhs, loc_sem.at[1])
    fac_in.start()
    rhs_in.start()

    barrier = pltpu.get_barrier_semaphore()

    def greet_row(p):
        @pl.when(p != r)
        def _():
            pl.semaphore_signal(barrier, inc=1, device_id=(p, c), device_id_type=MESH)

    def greet_z(d):
        pl.semaphore_signal(barrier, inc=1, device_id=(r, 2 * zpeer(d) + core), device_id_type=MESH)

    loop(0, NR, greet_row)
    loop(1, NZ, greet_z)
    pl.semaphore_signal(barrier, inc=1, device_id=mate, device_id_type=MESH)

    rhs_in.wait()
    fac_in.wait()

    def compact(i):
        for q in range(2):
            own[q, i] = fac[pl.ds(i * 512 + q, 256, stride=2), :].reshape(16, 16, KB)

    loop(0, NZ, compact)
    py[...] = jnp.zeros_like(py)
    pl.semaphore_wait(barrier, NR - 1 + NZ - 1 + 1)

    def cols(p):
        return pl.ds(pl.multiple_of(p * KB, KB), KB)

    def slice_of(which, p, h):
        if which == 2:
            return own.at[1, pl.ds(4 * h, 4), p]
        return own.at[0, p // 2, pl.ds(p % 2 * 8 + 4 * h, 4)]

    def half(q, k, h):
        return w.at[q, k, pl.ds(4 * h, 4)]

    def sc_rhs(panel, p):
        dst = xs.at[0, p] if panel == 0 else r1
        return remote(rhs.at[:, cols(p)], dst, s_rhs.at[p], r_rhs.at[panel], (p, c))

    def source(which):
        return 0 if which == 0 else 1

    def far(which, p):
        return jnp.logical_and(p // NX == 2, p % NX != source(which))

    def sc_fac(which, p, h):
        return remote(slice_of(which, p, h), half(which, c, h), s_sc.at[which, h, p], r_sc.at[which, h], (p, c))

    def sc_far(which, p, h):
        to = rel.at[which, pl.ds(4 * h, 4)]
        return remote(slice_of(which, p, h), to, s_sc.at[which, h, p], r_rel.at[which, h], (p % NX, c))

    def relay(which, h):
        got = rel.at[which, pl.ds(4 * h, 4)]
        return remote(got, half(which, c, h), s_rel.at[which, h], r_sc.at[which, h], ((r + 2 * NX) % NR, c))

    def sc_fac_go(which, h, act):
        def step(d):
            p = rowpeer(d)
            f = far(which, p)

            @pl.when(f)
            def _():
                act(sc_far(which, p, h))

            @pl.when(jnp.logical_not(f))
            def _():
                act(sc_fac(which, p, h))

        loop(1, NR, step)

    def sc_fac_start(which):
        for h in range(2):
            sc_fac_go(which, h, lambda cp: cp.start())

    def sc_fac_left(which):
        for h in range(2):
            sc_fac_go(which, h, lambda cp: cp.wait_send())

    def is_relay(which):
        return jnp.logical_and(r < NX, r != source(which))

    def relay_go(which, h):
        @pl.when(is_relay(which))
        def _():
            got = rel.at[which, pl.ds(4 * h, 4)]
            remote(got, got, s_rel.at[which, h], r_rel.at[which, h], (rowpeer(1), c)).wait_recv()
            relay(which, h).start()

    def rhs_start(panel):
        @pl.when(r == panel)
        def _():
            loop(1, NR, lambda d: sc_rhs(panel, rowpeer(d)).start())

    def last_start():
        @pl.when(r == 1)
        def _():
            sc_fac_start(2)

    @pl.when(r == 0)
    def _():
        sc_fac_start(0)
        xs[0, 0] = rhs[:, 0:KB]
        w[0, c] = own[0, 0, 0:8]

    @pl.when(r == 1)
    def _():
        sc_fac_start(1)
        r1[...] = rhs[:, KB : 2 * KB]
        w[1, c] = own[0, 0, 8:16]
        w[2, c] = own[1, :, 1]

    def swap(q):
        return remote(own.at[q], other.at[q], s_l.at[q], r_l.at[q], mate)

    for q in range(2):
        swap(q).start()

    def convert(src, lane):
        def step(i):
            at = pl.ds(pl.multiple_of(i * 256, 256), 256)
            for q in range(2):
                hi, lo = split(src[q, i].reshape(256, KB))
                lhi[q, at, cols(lane)] = hi
                llo[q, at, cols(lane)] = lo

        loop(0, NZ, step)

    def ag(b, d):
        return remote(xs.at[b, r], xs.at[b, r], s_ag.at[b, d], r_ag.at[b, r], (rowpeer(d), c))

    def ag_in(b, d):
        p = rowpeer(d)
        return remote(xs.at[b, p], xs.at[b, p], s_ag.at[b, d], r_ag.at[b, p], (p, c))

    def ag_start(b):
        loop(1, NR, lambda d: ag(b, d).start())

    def ag_wait(b):
        loop(1, NR, lambda d: ag_in(b, d).wait_recv())

    def zcopy(q, h, i, far_z, d):
        k = 2 * far_z + core
        return remote(half(q, k, h), half(q, k, h), s_z.at[q, h, i], r_z.at[q, h, far_z], (r, 2 * zpeer(d) + core))

    def zfirst(q, h):
        return [zcopy(q, h, i, z, d) for i, d in enumerate((2, NZ - 2, 1, NZ - 1))]

    def zsecond(q, h):
        left, right = zpeer(NZ - 2), zpeer(2)
        last = zcopy(q, h, 6, left, 2) if h == 0 else zcopy(q, h, 6, right, NZ - 2)
        return [last, zcopy(q, h, 4, left, 1), zcopy(q, h, 5, right, NZ - 1)]

    def zin(q, h, d):
        zcopy(q, h, 0, zpeer(d), 1).wait_recv()

    def xsend(q, d):
        k = 2 * zpeer(d) + core
        return remote(w.at[q, k], w.at[q, k], s_cx.at[q, d], r_cx.at[q, zpeer(d)], mate)

    def xrecv(q, d):
        k = 2 * zpeer(d) + 1 - core
        return remote(w.at[q, k], w.at[q, k], s_cx.at[q, d], r_cx.at[q, zpeer(d)], mate)

    def ready(q, k):
        hi, lo = split(w[q, k].reshape(KB, KB))
        at = cols(k)
        wb[q, 0:KB, at] = hi
        wb[q, KB : 2 * KB, at] = lo

    def slice_in(q, h):
        @pl.when(r != source(q))
        def _():
            remote(half(q, c, h), half(q, c, h), s_rhs.at[0], r_sc.at[q, h], (rowpeer(1), c)).wait_recv()

    def fetch(q):
        for h in range(2):
            relay_go(q, h)
            slice_in(q, h)
            for cp in zfirst(q, h):
                cp.start()
        xsend(q, 0).start()
        ready(q, c)

    def hand_on(q, h):
        zin(q, h, 2)
        zin(q, h, NZ - 2)
        for cp in zsecond(q, h):
            cp.start()

    def near(q):
        for d in (2, NZ - 2):
            xsend(q, d).start()
            ready(q, 2 * zpeer(d) + core)
        arrive(q, (1, NZ - 1))

    def arrive(q, which):
        for d in which:
            for h in range(2):
                zin(q, h, d)
            xsend(q, d).start()
            ready(q, 2 * zpeer(d) + core)

    def collect(q):
        def step(d):
            xrecv(q, d).wait_recv()
            ready(q, 2 * zpeer(d) + 1 - core)

        loop(0, NZ, step)

    def load_x(b):
        def step(k):
            hi, lo = split(xs[b, k])
            xb[0:MB, cols(k)] = hi
            xb[MB : 2 * MB, cols(k)] = lo

        loop(0, NR, step)

    def product(q):
        o = dot_nt(xb[...], wb[q])
        return o[0:MB, 0:KB] + o[MB : 2 * MB, 0:KB] + o[0:MB, KB : 2 * KB]

    def rhs0_in():
        @pl.when(r != 0)
        def _():
            remote(xs.at[0, r], xs.at[0, r], s_rhs.at[0], r_rhs.at[0], (rowpeer(1), c)).wait_recv()

    def rhs1_in():
        @pl.when(r != 1)
        def _():
            remote(r1, r1, s_rhs.at[0], r_rhs.at[1], (rowpeer(1), c)).wait_recv()

    def swap_in():
        for q in range(2):
            swap(q).wait_recv()

    def zorder(i):
        h = (i + 1) // 2
        return h + (i + 1) % 2 * (NZ - 2 * h)

    def a2a(d):
        p = zpeer(d)
        return remote(xs.at[1, pl.ds(2 * p, 2)], t.at[z], s_a.at[0, d], r_a.at[0, z], (r, 2 * p + core))

    def a2a_from(p):
        d = 1
        return remote(t.at[p], t.at[p], s_a.at[0, d], r_a.at[0, p], (r, 2 * p + core))

    def regroup(d):
        p = zpeer(d)
        return remote(py.at[p], pz.at[z], s_a.at[1, d], r_a.at[1, z], (r, 2 * p + core))

    def regroup_in(d):
        p = zpeer(d)
        return remote(pz.at[p], pz.at[p], s_a.at[1, d], r_a.at[1, p], (r, 2 * p + core))

    def spread(g, d):
        return remote(gx.at[g, r], gx.at[g, r], s_g.at[g, d], r_g.at[g, r], (rowpeer(d), c))

    def spread_in(g, d):
        p = rowpeer(d)
        return remote(gx.at[g, p], gx.at[g, p], s_g.at[g, d], r_g.at[g, p], (p, c))

    def to_owner():
        return remote(py, s1t.at[:, r], s_o, r_o.at[r], (1, c))

    def from_peer(d):
        p = rowpeer(d)
        return remote(py, s1t.at[:, p], s_o, r_o.at[p], (p, c))

    def dest(way, s):
        return (z + NZ - 1 - s) % NZ if way == 0 else (z + 1 + s) % NZ

    def hop(way, s, j):
        lanes = pl.ds(way * HALF + j * PIECE, PIECE)
        to = (z + 1) % NZ if way == 0 else (z + NZ - 1) % NZ
        return remote(
            acc.at[dest(way, s), :, lanes], slots.at[way, s, j], s_rs.at[way, s, j], r_rs.at[way, s, j],
            (r, 2 * to + core),
        )

    def left_scatter():
        @pl.when(r == 0)
        def _():
            loop(1, NR, lambda d: sc_rhs(0, rowpeer(d)).wait_send())
            sc_fac_left(0)

        @pl.when(r == 1)
        def _():
            loop(1, NR, lambda d: sc_rhs(1, rowpeer(d)).wait_send())
            sc_fac_left(1)
            sc_fac_left(2)

        for which in range(3):

            @pl.when(is_relay(which))
            def _(which=which):
                for h in range(2):
                    relay(which, h).wait_send()

    def left_swap():
        for q in range(2):
            swap(q).wait_send()

    def left_f(q):
        for h in range(2):
            for cp in zfirst(q, h) + zsecond(q, h):
                cp.wait_send()
        loop(0, NZ, lambda d: xsend(q, d).wait_send())

    def left_ag(b):
        loop(1, NR, lambda d: ag(b, d).wait_send())

    def left_a2a():
        loop(1, NZ, lambda d: a2a(d).wait_send())

    def left_regroup():
        loop(1, NZ, lambda d: regroup(d).wait_send())

    def left_spread():
        loop(1, NR, lambda d: spread(1, d).wait_send())

    def left_ring():
        def drain(s):
            for way in range(2):
                for j in range(SUB):
                    hop(way, s, j).wait_send()

        loop(0, NZ - 1, drain)

    convert(own, core)
    fetch(0)
    rhs_start(0)
    fetch(1)
    rhs0_in()
    ag_start(0)
    hand_on(0, 0)
    hand_on(0, 1)
    last_start()
    near(0)
    hand_on(1, 0)
    hand_on(1, 1)
    arrive(0, (3, NZ - 3, 4))
    rhs_start(1)
    near(1)
    fetch(2)
    ag_wait(0)
    load_x(0)
    collect(0)
    xs[1, r] = product(0)
    ag_start(1)
    hand_on(2, 0)
    hand_on(2, 1)
    arrive(1, (3, NZ - 3, 4))
    swap_in()
    convert(other, 1 - core)
    near(2)
    arrive(2, (3, NZ - 3, 4))
    ag_wait(1)
    load_x(1)
    collect(1)
    rhs1_in()
    xs[2, r] = r1[...] - product(1)
    ag_start(2)
    loop(1, NZ, lambda d: a2a(d).start())
    t[z] = xs[1, pl.ds(2 * z, 2)]
    ag_wait(2)
    collect(2)
    load_x(2)
    turned = dot_nt(wb[2], xb[0:MB, :])
    turned = turned[0:KB] + turned[KB : 2 * KB] + dot_nt(wb[2, 0:KB, :], xb[MB : 2 * MB, :])
    py[:, :, 0:MB] = turned.reshape(NZ, 16, MB)
    loop(1, NZ, lambda d: regroup(d).start())
    pz[z] = py[z]

    loop(1, NZ, lambda d: regroup_in(d).wait_recv())

    def pair(g):
        return (z + NZ - 1 - g) % NZ, z if g == 3 else (z + 1 + g) % NZ

    def spread_start(g):
        for i in range(2):
            one, two = pair(2 * g + i)
            gx[g, r, i] = pz[one] + pltpu.roll(pz[two], MB, 1)
        loop(1, NR, lambda d: spread(g, d).start())

    def spread_end(g):
        loop(1, NR, lambda d: spread_in(g, d).wait_recv())
        for n in range(2):
            for k in range(2):
                hi, lo = split(gx[g, 8 * k : 8 * k + 8, n].reshape(KB, KB).T)
                for i, d in enumerate(pair(2 * g + n)):
                    rows = pl.ds(pl.multiple_of(d * MB, MB), MB)
                    tb[0, rows, k * KB : (k + 1) * KB] = hi[i * MB : (i + 1) * MB]
                    tb[1, rows, k * KB : (k + 1) * KB] = lo[i * MB : (i + 1) * MB]

    spread_start(0)

    def first_in(d, away):
        if away:
            a2a_from(d).wait_recv()
        rows = pl.ds(pl.multiple_of(d * MB, MB), MB)
        for k in range(2):
            hi, lo = split(t[d, k])
            ta[0, rows, k * KB : (k + 1) * KB] = hi
            ta[1, rows, k * KB : (k + 1) * KB] = lo

    def first_in_step(s):
        first_in(dest(0, s), True)
        first_in(z if s == 3 else dest(1, s), s != 3)

    def part(q, way, s):
        d = dest(way, s)
        rows = pl.ds(pl.multiple_of(d * MB, MB), MB)
        from_ = ta if q == 0 else tb
        hi, lo = from_[0, rows, :], from_[1, rows, :]
        for j in range(HALF // 512):
            at = slice(way * HALF + j * 512, way * HALF + (j + 1) * 512)
            o = dot_nt(jnp.concatenate([hi, lo], axis=0), lhi[q, at, :])
            o = o[0:MB] + o[MB : 2 * MB] + dot_nt(hi, llo[q, at, :])
            if q == 0:
                acc[d, :, at] = o
            else:
                acc[d, :, at] += o

    def parts(q, s):
        for way in range(2):
            part(q, way, s)

    def pass_on(way, s, j):
        @pl.when(jnp.int32(s) < NZ - 1)
        def _():
            hop(way, s, j).start()

    def ring(s):
        if isinstance(s, int) and s == 1:
            spread_end(1)
            parts(1, 2)
        for j in range(SUB):
            for way in range(2):
                lanes = slice(way * HALF + j * PIECE, way * HALF + (j + 1) * PIECE)
                hop(way, s, j).wait_recv()
                acc[dest(way, s + 1), :, lanes] += slots[way, s, j]
                pass_on(way, s + 1, j)
            if isinstance(s, int) and s == 6:
                continue
            if j == 0:
                if isinstance(s, int) and s < 2:
                    first_in_step(s + 2)
                parts(0, s + 2)
            if j == SUB - 1:
                if isinstance(s, int) and s == 0:
                    continue
                parts(1, s + 2)

    for s in range(2):
        first_in_step(s)
        parts(0, s)
    loop(1, NR, lambda d: spread(0, d).wait_send())
    spread_start(1)
    spread_end(0)
    for way in range(2):
        part(1, way, 0)
        for j in range(SUB):
            hop(way, 0, j).start()
    parts(1, 1)

    @pl.when(r != 1)
    def _():
        to_owner().start()

    @pl.when(r == 1)
    def _():
        s1t[:, 1] = py[...]


    for s in range(2):
        ring(s)
    loop(2, NZ - 2, ring)
    ring(NZ - 2)

    @pl.when(r == 0)
    def _():
        for k in range(NR):
            out_ref[:, k * KB : (k + 1) * KB] = xs[1, k]

    @pl.when(r == 1)
    def _():
        loop(1, NR, lambda d: from_peer(d).wait_recv())
        for k in range(NR):
            block = s1t[k // 2, k % 2 * 8 : k % 2 * 8 + 8].reshape(KB, KB)
            out_ref[:, k * KB : (k + 1) * KB] = block.T[0:MB]

    @pl.when(r > 1)
    def _():
        out_ref[...] = rhs[...] - acc[z]

    @pl.when(r != 1)
    def _():
        to_owner().wait_send()

    left_scatter()
    left_swap()
    for q in range(3):
        left_f(q)
        left_ag(q)
    left_a2a()
    left_regroup()
    left_spread()
    left_ring()


def local(right_side, factor):
    rows = factor.shape[0]
    dma = pltpu.SemaphoreType.DMA
    return pl.pallas_call(
        kernel,
        name="panels",
        out_shape=jax.ShapeDtypeStruct((MB, NB), F32),
        in_specs=[pl.BlockSpec(memory_space=pl.ANY)] * 2,
        out_specs=pl.BlockSpec(memory_space=pltpu.VMEM),
        scratch_shapes=[
            pltpu.VMEM((2 * NB, KB), F32),
            pltpu.VMEM((MB, NB), F32),
            pltpu.VMEM((2, NZ, 16, 16, KB), F32),
            pltpu.VMEM((2, NZ, 16, 16, KB), F32),
            pltpu.VMEM((2, NB, 2 * KB), BF16),
            pltpu.VMEM((2, NB, 2 * KB), BF16),
            pltpu.VMEM((3, 16, 8, 16, KB), F32),
            pltpu.VMEM((3, 8, 16, KB), F32),
            pltpu.VMEM((3, 2 * KB, NB), BF16),
            pltpu.VMEM((3, NR, MB, KB), F32),
            pltpu.VMEM((MB, KB), F32),
            pltpu.VMEM((2 * MB, NB), BF16),
            pltpu.VMEM((NZ, 2, MB, KB), F32),
            pltpu.VMEM((NZ, 16, KB), F32),
            pltpu.VMEM((NZ, 16, KB), F32),
            pltpu.VMEM((2, NR, 2, 16, KB), F32),
            pltpu.VMEM((NZ, NR, 16, KB), F32),
            pltpu.VMEM((2, MC, 2 * KB), BF16),
            pltpu.VMEM((2, MC, 2 * KB), BF16),
            pltpu.VMEM((NZ, MB, NB), F32),
            pltpu.VMEM((2, NZ - 1, SUB, MB, PIECE), F32),
            dma((2,)),
            dma((NR,)),
            dma((2,)),
            dma((3, 2, NR)),
            dma((3, 2)),
            dma((3, 2)),
            dma((3, 2)),
            dma((3, 2, 7)),
            dma((3, 2, NZ)),
            dma((3, NZ)),
            dma((3, NZ)),
            dma((3, NR)),
            dma((3, NR)),
            dma((2, NZ)),
            dma((2, NZ)),
            dma((2, NR)),
            dma((2, NR)),
            dma,
            dma((NR,)),
            dma((2,)),
            dma((2,)),
            dma((2, NZ - 1, SUB)),
            dma((2, NZ - 1, SUB)),
        ],
        compiler_params=pltpu.CompilerParams(
            collective_id=0, has_side_effects=True, vmem_limit_bytes=60 * 2**20
        ),
    )(right_side, factor.reshape(2 * rows, KB))


def solution(mesh):
    in_specs = (P("col", "row"), P("row", None, "col"))
    out_specs = P("col", "row")
    return jax.shard_map(local, mesh=mesh, in_specs=in_specs, out_specs=out_specs, check_vma=False)
```

```python
import jax
import jax.numpy as jnp
from jax import lax
from jax.experimental import pallas as pl
from jax.experimental.pallas import tpu as pltpu
from jax.sharding import PartitionSpec as P

STOP = 99
MESH = pl.DeviceIdType.MESH
F32, BF16 = jnp.float32, jnp.bfloat16
NR = 16
NX = 4
NZ = 8
NB = 2048
MB = 48
KB = 128
MC = NZ * MB
SUB = 4
HALF = NB // 2
PIECE = HALF // SUB


def split(x):
    hi = x.astype(BF16)
    return hi, (x - hi.astype(F32)).astype(BF16)


def dot_nt(a, b):
    return lax.dot_general(a, b, (((1,), (1,)), ((), ())), preferred_element_type=F32)


def remote(src, dst, ssem, rsem, dev):
    return pltpu.make_async_remote_copy(
        src_ref=src, dst_ref=dst, send_sem=ssem, recv_sem=rsem, device_id=dev, device_id_type=MESH
    )


def loop(lo, hi, body):
    def step(i, carry):
        body(i)
        return carry

    lax.fori_loop(lo, hi, step, 0)


def kernel(
    rhs_hbm, fac_hbm, out_ref,
    fac, rhs, own, other, lhi, llo, w, rel, wb, xs, r1, xb, t, py, pz, gx, s1t, ta, tb, acc, slots,
    loc_sem, s_rhs, r_rhs, s_sc, r_sc, s_rel, r_rel, s_z, r_z, s_cx, r_cx, s_ag, r_ag, s_a, r_a, s_g, r_g, s_o, r_o,
    s_l, r_l, s_rs, r_rs,
):
    r = lax.axis_index("row")
    c = lax.axis_index("col")
    z = c // 2
    core = c % 2
    mate = (r, c + 1 - 2 * core)

    def rowpeer(d):
        return (r + d) % NR

    def zpeer(d):
        return (z + d) % NZ

    fac_in = pltpu.make_async_copy(fac_hbm, fac, loc_sem.at[0])
    rhs_in = pltpu.make_async_copy(rhs_hbm, rhs, loc_sem.at[1])
    fac_in.start()
    rhs_in.start()

    barrier = pltpu.get_barrier_semaphore()

    def greet_row(p):
        @pl.when(p != r)
        def _():
            pl.semaphore_signal(barrier, inc=1, device_id=(p, c), device_id_type=MESH)

    def greet_z(d):
        pl.semaphore_signal(barrier, inc=1, device_id=(r, 2 * zpeer(d) + core), device_id_type=MESH)

    loop(0, NR, greet_row)
    loop(1, NZ, greet_z)
    pl.semaphore_signal(barrier, inc=1, device_id=mate, device_id_type=MESH)

    rhs_in.wait()
    fac_in.wait()

    def compact(i):
        for q in range(2):
            own[q, i] = fac[pl.ds(i * 512 + q, 256, stride=2), :].reshape(16, 16, KB)

    loop(0, NZ, compact)
    py[...] = jnp.zeros_like(py)
    pl.semaphore_wait(barrier, NR - 1 + NZ - 1 + 1)

    def cols(p):
        return pl.ds(pl.multiple_of(p * KB, KB), KB)

    def slice_of(which, p, h):
        if which == 2:
            return own.at[1, pl.ds(4 * h, 4), p]
        return own.at[0, p // 2, pl.ds(p % 2 * 8 + 4 * h, 4)]

    def half(q, k, h):
        return w.at[q, k, pl.ds(4 * h, 4)]

    def sc_rhs(panel, p):
        dst = xs.at[0, p] if panel == 0 else r1
        return remote(rhs.at[:, cols(p)], dst, s_rhs.at[p], r_rhs.at[panel], (p, c))

    def source(which):
        return 0 if which == 0 else 1

    def far(which, p):
        return jnp.logical_and(p // NX == 2, p % NX != source(which))

    def sc_fac(which, p, h):
        return remote(slice_of(which, p, h), half(which, c, h), s_sc.at[which, h, p], r_sc.at[which, h], (p, c))

    def sc_far(which, p, h):
        to = rel.at[which, pl.ds(4 * h, 4)]
        return remote(slice_of(which, p, h), to, s_sc.at[which, h, p], r_rel.at[which, h], (p % NX, c))

    def relay(which, h):
        got = rel.at[which, pl.ds(4 * h, 4)]
        return remote(got, half(which, c, h), s_rel.at[which, h], r_sc.at[which, h], ((r + 2 * NX) % NR, c))

    def sc_fac_go(which, h, act):
        def step(d):
            p = rowpeer(d)
            f = far(which, p)

            @pl.when(f)
            def _():
                act(sc_far(which, p, h))

            @pl.when(jnp.logical_not(f))
            def _():
                act(sc_fac(which, p, h))

        loop(1, NR, step)

    def sc_fac_start(which):
        for h in range(2):
            sc_fac_go(which, h, lambda cp: cp.start())

    def sc_fac_left(which):
        for h in range(2):
            sc_fac_go(which, h, lambda cp: cp.wait_send())

    def is_relay(which):
        return jnp.logical_and(r < NX, r != source(which))

    def relay_go(which, h):
        @pl.when(is_relay(which))
        def _():
            got = rel.at[which, pl.ds(4 * h, 4)]
            remote(got, got, s_rel.at[which, h], r_rel.at[which, h], (rowpeer(1), c)).wait_recv()
            relay(which, h).start()

    def rhs_start(panel):
        @pl.when(r == panel)
        def _():
            loop(1, NR, lambda d: sc_rhs(panel, rowpeer(d)).start())

    def last_start():
        @pl.when(r == 1)
        def _():
            sc_fac_start(2)

    @pl.when(r == 0)
    def _():
        sc_fac_start(0)
        xs[0, 0] = rhs[:, 0:KB]
        w[0, c] = own[0, 0, 0:8]

    @pl.when(r == 1)
    def _():
        sc_fac_start(1)
        r1[...] = rhs[:, KB : 2 * KB]
        w[1, c] = own[0, 0, 8:16]
        w[2, c] = own[1, :, 1]

    def swap(q):
        return remote(own.at[q], other.at[q], s_l.at[q], r_l.at[q], mate)

    for q in range(2):
        swap(q).start()

    def convert(src, lane):
        def step(i):
            at = pl.ds(pl.multiple_of(i * 256, 256), 256)
            for q in range(2):
                hi, lo = split(src[q, i].reshape(256, KB))
                lhi[q, at, cols(lane)] = hi
                llo[q, at, cols(lane)] = lo

        loop(0, NZ, step)

    def ag(b, d):
        return remote(xs.at[b, r], xs.at[b, r], s_ag.at[b, d], r_ag.at[b, r], (rowpeer(d), c))

    def ag_in(b, d):
        p = rowpeer(d)
        return remote(xs.at[b, p], xs.at[b, p], s_ag.at[b, d], r_ag.at[b, p], (p, c))

    def ag_start(b):
        loop(1, NR, lambda d: ag(b, d).start())

    def ag_wait(b):
        loop(1, NR, lambda d: ag_in(b, d).wait_recv())

    def zcopy(q, h, i, far_z, d):
        k = 2 * far_z + core
        return remote(half(q, k, h), half(q, k, h), s_z.at[q, h, i], r_z.at[q, h, far_z], (r, 2 * zpeer(d) + core))

    def zfirst(q, h):
        return [zcopy(q, h, i, z, d) for i, d in enumerate((2, NZ - 2, 1, NZ - 1))]

    def zsecond(q, h):
        left, right = zpeer(NZ - 2), zpeer(2)
        last = zcopy(q, h, 6, left, 2) if h == 0 else zcopy(q, h, 6, right, NZ - 2)
        return [last, zcopy(q, h, 4, left, 1), zcopy(q, h, 5, right, NZ - 1)]

    def zin(q, h, d):
        zcopy(q, h, 0, zpeer(d), 1).wait_recv()

    def xsend(q, d):
        k = 2 * zpeer(d) + core
        return remote(w.at[q, k], w.at[q, k], s_cx.at[q, d], r_cx.at[q, zpeer(d)], mate)

    def xrecv(q, d):
        k = 2 * zpeer(d) + 1 - core
        return remote(w.at[q, k], w.at[q, k], s_cx.at[q, d], r_cx.at[q, zpeer(d)], mate)

    def ready(q, k):
        hi, lo = split(w[q, k].reshape(KB, KB))
        at = cols(k)
        wb[q, 0:KB, at] = hi
        wb[q, KB : 2 * KB, at] = lo

    def slice_in(q, h):
        @pl.when(r != source(q))
        def _():
            remote(half(q, c, h), half(q, c, h), s_rhs.at[0], r_sc.at[q, h], (rowpeer(1), c)).wait_recv()

    def fetch(q):
        for h in range(2):
            relay_go(q, h)
            slice_in(q, h)
            for cp in zfirst(q, h):
                cp.start()
        xsend(q, 0).start()
        ready(q, c)

    def hand_on(q, h):
        zin(q, h, 2)
        zin(q, h, NZ - 2)
        for cp in zsecond(q, h):
            cp.start()

    def near(q):
        for d in (2, NZ - 2):
            xsend(q, d).start()
            ready(q, 2 * zpeer(d) + core)
        arrive(q, (1, NZ - 1))

    def arrive(q, which):
        for d in which:
            for h in range(2):
                zin(q, h, d)
            xsend(q, d).start()
            ready(q, 2 * zpeer(d) + core)

    def collect(q):
        def step(d):
            xrecv(q, d).wait_recv()
            ready(q, 2 * zpeer(d) + 1 - core)

        loop(0, NZ, step)

    def load_x(b):
        def step(k):
            hi, lo = split(xs[b, k])
            xb[0:MB, cols(k)] = hi
            xb[MB : 2 * MB, cols(k)] = lo

        loop(0, NR, step)

    def product(q):
        o = dot_nt(xb[...], wb[q])
        return o[0:MB, 0:KB] + o[MB : 2 * MB, 0:KB] + o[0:MB, KB : 2 * KB]

    def rhs0_in():
        @pl.when(r != 0)
        def _():
            remote(xs.at[0, r], xs.at[0, r], s_rhs.at[0], r_rhs.at[0], (rowpeer(1), c)).wait_recv()

    def rhs1_in():
        @pl.when(r != 1)
        def _():
            remote(r1, r1, s_rhs.at[0], r_rhs.at[1], (rowpeer(1), c)).wait_recv()

    def swap_in():
        for q in range(2):
            swap(q).wait_recv()

    def zorder(i):
        h = (i + 1) // 2
        return h + (i + 1) % 2 * (NZ - 2 * h)

    def a2a(d):
        p = zpeer(d)
        return remote(xs.at[1, pl.ds(2 * p, 2)], t.at[z], s_a.at[0, d], r_a.at[0, z], (r, 2 * p + core))

    def a2a_from(p):
        d = 1
        return remote(t.at[p], t.at[p], s_a.at[0, d], r_a.at[0, p], (r, 2 * p + core))

    def regroup(d):
        p = zpeer(d)
        return remote(py.at[p], pz.at[z], s_a.at[1, d], r_a.at[1, z], (r, 2 * p + core))

    def regroup_in(d):
        p = zpeer(d)
        return remote(pz.at[p], pz.at[p], s_a.at[1, d], r_a.at[1, p], (r, 2 * p + core))

    def spread(g, d):
        return remote(gx.at[g, r], gx.at[g, r], s_g.at[g, d], r_g.at[g, r], (rowpeer(d), c))

    def spread_in(g, d):
        p = rowpeer(d)
        return remote(gx.at[g, p], gx.at[g, p], s_g.at[g, d], r_g.at[g, p], (p, c))

    def to_owner():
        return remote(py, s1t.at[:, r], s_o, r_o.at[r], (1, c))

    def from_peer(d):
        p = rowpeer(d)
        return remote(py, s1t.at[:, p], s_o, r_o.at[p], (p, c))

    def dest(way, s):
        return (z + NZ - 1 - s) % NZ if way == 0 else (z + 1 + s) % NZ

    def hop(way, s, j):
        lanes = pl.ds(way * HALF + j * PIECE, PIECE)
        to = (z + 1) % NZ if way == 0 else (z + NZ - 1) % NZ
        return remote(
            acc.at[dest(way, s), :, lanes], slots.at[way, s, j], s_rs.at[way, s, j], r_rs.at[way, s, j],
            (r, 2 * to + core),
        )

    def left_scatter():
        @pl.when(r == 0)
        def _():
            loop(1, NR, lambda d: sc_rhs(0, rowpeer(d)).wait_send())
            sc_fac_left(0)

        @pl.when(r == 1)
        def _():
            loop(1, NR, lambda d: sc_rhs(1, rowpeer(d)).wait_send())
            sc_fac_left(1)
            sc_fac_left(2)

        for which in range(3):

            @pl.when(is_relay(which))
            def _(which=which):
                for h in range(2):
                    relay(which, h).wait_send()

    def left_swap():
        for q in range(2):
            swap(q).wait_send()

    def left_f(q):
        for h in range(2):
            for cp in zfirst(q, h) + zsecond(q, h):
                cp.wait_send()
        loop(0, NZ, lambda d: xsend(q, d).wait_send())

    def left_ag(b):
        loop(1, NR, lambda d: ag(b, d).wait_send())

    def left_a2a():
        loop(1, NZ, lambda d: a2a(d).wait_send())

    def left_regroup():
        loop(1, NZ, lambda d: regroup(d).wait_send())

    def left_spread():
        loop(1, NR, lambda d: spread(1, d).wait_send())

    def drain(s):
        for way in range(2):
            for j in range(SUB):
                hop(way, s, j).wait_send()

    convert(own, core)
    fetch(0)
    rhs_start(0)
    fetch(1)
    last_start()
    rhs_start(1)
    hand_on(0, 0)
    hand_on(0, 1)
    rhs0_in()
    ag_start(0)
    near(0)
    hand_on(1, 0)
    hand_on(1, 1)
    arrive(0, (3, NZ - 3, 4))
    near(1)
    fetch(2)
    ag_wait(0)
    load_x(0)
    collect(0)
    xs[1, r] = product(0)
    ag_start(1)
    hand_on(2, 0)
    hand_on(2, 1)
    arrive(1, (3, NZ - 3, 4))
    swap_in()
    convert(other, 1 - core)
    near(2)
    arrive(2, (3, NZ - 3, 4))
    ag_wait(1)
    load_x(1)
    collect(1)
    rhs1_in()
    xs[2, r] = r1[...] - product(1)
    ag_start(2)
    loop(1, NZ, lambda d: a2a(d).start())
    t[z] = xs[1, pl.ds(2 * z, 2)]
    left_swap()
    for q in range(2):
        left_f(q)
        left_ag(q)
    ag_wait(2)
    collect(2)
    load_x(2)
    turned = dot_nt(wb[2], xb[0:MB, :])
    turned = turned[0:KB] + turned[KB : 2 * KB] + dot_nt(wb[2, 0:KB, :], xb[MB : 2 * MB, :])
    py[:, :, 0:MB] = turned.reshape(NZ, 16, MB)
    loop(1, NZ, lambda d: regroup(d).start())
    pz[z] = py[z]

    left_f(2)
    left_ag(2)
    loop(1, NZ, lambda d: regroup_in(d).wait_recv())

    def pair(g):
        return (z + NZ - 1 - g) % NZ, z if g == 3 else (z + 1 + g) % NZ

    def spread_start(g):
        for i in range(2):
            one, two = pair(2 * g + i)
            gx[g, r, i] = pz[one] + pltpu.roll(pz[two], MB, 1)
        loop(1, NR, lambda d: spread(g, d).start())

    def spread_end(g):
        loop(1, NR, lambda d: spread_in(g, d).wait_recv())
        for n in range(2):
            for k in range(2):
                hi, lo = split(gx[g, 8 * k : 8 * k + 8, n].reshape(KB, KB).T)
                for i, d in enumerate(pair(2 * g + n)):
                    rows = pl.ds(pl.multiple_of(d * MB, MB), MB)
                    tb[0, rows, k * KB : (k + 1) * KB] = hi[i * MB : (i + 1) * MB]
                    tb[1, rows, k * KB : (k + 1) * KB] = lo[i * MB : (i + 1) * MB]

    spread_start(0)

    def first_in(d, away):
        if away:
            a2a_from(d).wait_recv()
        rows = pl.ds(pl.multiple_of(d * MB, MB), MB)
        for k in range(2):
            hi, lo = split(t[d, k])
            ta[0, rows, k * KB : (k + 1) * KB] = hi
            ta[1, rows, k * KB : (k + 1) * KB] = lo

    def first_in_step(s):
        first_in(dest(0, s), True)
        first_in(z if s == 3 else dest(1, s), s != 3)

    def part(q, way, s):
        d = dest(way, s)
        rows = pl.ds(pl.multiple_of(d * MB, MB), MB)
        from_ = ta if q == 0 else tb
        hi, lo = from_[0, rows, :], from_[1, rows, :]
        for j in range(HALF // 512):
            at = slice(way * HALF + j * 512, way * HALF + (j + 1) * 512)
            o = dot_nt(jnp.concatenate([hi, lo], axis=0), lhi[q, at, :])
            o = o[0:MB] + o[MB : 2 * MB] + dot_nt(hi, llo[q, at, :])
            if q == 0:
                acc[d, :, at] = o
            else:
                acc[d, :, at] += o

    def parts(q, s):
        for way in range(2):
            part(q, way, s)

    def pass_on(way, s, j):
        @pl.when(jnp.int32(s) < NZ - 1)
        def _():
            hop(way, s, j).start()

    def ring(s):
        if isinstance(s, int) and s == 1:
            spread_end(1)
            parts(1, 2)
        for j in range(SUB):
            for way in range(2):
                lanes = slice(way * HALF + j * PIECE, way * HALF + (j + 1) * PIECE)
                hop(way, s, j).wait_recv()
                acc[dest(way, s + 1), :, lanes] += slots[way, s, j]
                pass_on(way, s + 1, j)
            if j == 1 and not (isinstance(s, int) and s == 0):
                drain(s - 1)
            if isinstance(s, int) and s == 6:
                continue
            if j == 0:
                if isinstance(s, int) and s < 2:
                    first_in_step(s + 2)
                parts(0, s + 2)
            if j == SUB - 1:
                if isinstance(s, int) and s == 0:
                    continue
                parts(1, s + 2)

    for s in range(2):
        first_in_step(s)
        parts(0, s)
    loop(1, NR, lambda d: spread(0, d).wait_send())
    spread_start(1)
    spread_end(0)

    def left_late():
        left_a2a()
        left_regroup()
        left_spread()

    @pl.when(r > 1)
    def _():
        for way in range(2):
            part(1, way, 0)
            for j in range(SUB):
                hop(way, 0, j).start()
        parts(1, 1)
        left_late()
        ring(0)
        ring(1)
        to_owner().start()
        loop(2, NZ - 2, ring)
        ring(NZ - 2)
        out_ref[...] = rhs[...] - acc[z]
        to_owner().wait_send()
        drain(NZ - 2)

    def no_ring():
        spread_end(1)
        first_in_step(2)
        first_in_step(3)
        left_late()

    @pl.when(r == 0)
    def _():
        no_ring()
        to_owner().start()
        for k in range(NR):
            out_ref[:, k * KB : (k + 1) * KB] = xs[1, k]
        to_owner().wait_send()

    @pl.when(r == 1)
    def _():
        no_ring()
        s1t[:, 1] = py[...]
        loop(1, NR, lambda d: from_peer(d).wait_recv())
        for k in range(NR):
            block = s1t[k // 2, k % 2 * 8 : k % 2 * 8 + 8].reshape(KB, KB)
            out_ref[:, k * KB : (k + 1) * KB] = block.T[0:MB]

    left_scatter()


def local(right_side, factor):
    rows = factor.shape[0]
    dma = pltpu.SemaphoreType.DMA
    return pl.pallas_call(
        kernel,
        name="panels",
        out_shape=jax.ShapeDtypeStruct((MB, NB), F32),
        in_specs=[pl.BlockSpec(memory_space=pl.ANY)] * 2,
        out_specs=pl.BlockSpec(memory_space=pltpu.VMEM),
        scratch_shapes=[
            pltpu.VMEM((2 * NB, KB), F32),
            pltpu.VMEM((MB, NB), F32),
            pltpu.VMEM((2, NZ, 16, 16, KB), F32),
            pltpu.VMEM((2, NZ, 16, 16, KB), F32),
            pltpu.VMEM((2, NB, 2 * KB), BF16),
            pltpu.VMEM((2, NB, 2 * KB), BF16),
            pltpu.VMEM((3, 16, 8, 16, KB), F32),
            pltpu.VMEM((3, 8, 16, KB), F32),
            pltpu.VMEM((3, 2 * KB, NB), BF16),
            pltpu.VMEM((3, NR, MB, KB), F32),
            pltpu.VMEM((MB, KB), F32),
            pltpu.VMEM((2 * MB, NB), BF16),
            pltpu.VMEM((NZ, 2, MB, KB), F32),
            pltpu.VMEM((NZ, 16, KB), F32),
            pltpu.VMEM((NZ, 16, KB), F32),
            pltpu.VMEM((2, NR, 2, 16, KB), F32),
            pltpu.VMEM((NZ, NR, 16, KB), F32),
            pltpu.VMEM((2, MC, 2 * KB), BF16),
            pltpu.VMEM((2, MC, 2 * KB), BF16),
            pltpu.VMEM((NZ, MB, NB), F32),
            pltpu.VMEM((2, NZ - 1, SUB, MB, PIECE), F32),
            dma((2,)),
            dma((NR,)),
            dma((2,)),
            dma((3, 2, NR)),
            dma((3, 2)),
            dma((3, 2)),
            dma((3, 2)),
            dma((3, 2, 7)),
            dma((3, 2, NZ)),
            dma((3, NZ)),
            dma((3, NZ)),
            dma((3, NR)),
            dma((3, NR)),
            dma((2, NZ)),
            dma((2, NZ)),
            dma((2, NR)),
            dma((2, NR)),
            dma,
            dma((NR,)),
            dma((2,)),
            dma((2,)),
            dma((2, NZ - 1, SUB)),
            dma((2, NZ - 1, SUB)),
        ],
        compiler_params=pltpu.CompilerParams(
            collective_id=0, has_side_effects=True, vmem_limit_bytes=60 * 2**20
        ),
    )(right_side, factor.reshape(2 * rows, KB))


def solution(mesh):
    in_specs = (P("col", "row"), P("row", None, "col"))
    out_specs = P("col", "row")
    return jax.shard_map(local, mesh=mesh, in_specs=in_specs, out_specs=out_specs, check_vma=False)
```

```python
import jax
import jax.numpy as jnp
from jax import lax
from jax.experimental import pallas as pl
from jax.experimental.pallas import tpu as pltpu
from jax.sharding import PartitionSpec as P

STOP = 99
MESH = pl.DeviceIdType.MESH
F32, BF16 = jnp.float32, jnp.bfloat16
NR = 16
NX = 4
NZ = 8
NB = 2048
MB = 48
KB = 128
MC = NZ * MB
SUB = 4
HALF = NB // 2
PIECE = HALF // SUB


def split(x):
    hi = x.astype(BF16)
    return hi, (x - hi.astype(F32)).astype(BF16)


def dot_nt(a, b):
    return lax.dot_general(a, b, (((1,), (1,)), ((), ())), preferred_element_type=F32)


def remote(src, dst, ssem, rsem, dev):
    return pltpu.make_async_remote_copy(
        src_ref=src, dst_ref=dst, send_sem=ssem, recv_sem=rsem, device_id=dev, device_id_type=MESH
    )


def loop(lo, hi, body):
    def step(i, carry):
        body(i)
        return carry

    lax.fori_loop(lo, hi, step, 0)


def kernel(
    rhs_hbm, fac_hbm, out_ref,
    fac, rhs, own, other, lhi, llo, w, rel, wb, xs, r1, xb, t, py, pz, gx, s1t, ta, tb, acc, slots,
    loc_sem, s_rhs, r_rhs, s_sc, r_sc, s_rel, r_rel, s_z, r_z, s_cx, r_cx, s_ag, r_ag, s_a, r_a, s_g, r_g, s_o, r_o,
    s_l, r_l, s_rs, r_rs,
):
    r = lax.axis_index("row")
    c = lax.axis_index("col")
    z = c // 2
    core = c % 2
    mate = (r, c + 1 - 2 * core)

    def rowpeer(d):
        return (r + d * (7 + 2 * core)) % NR

    def zpeer(d):
        return (z + d) % NZ

    fac_in = pltpu.make_async_copy(fac_hbm, fac, loc_sem.at[0])
    rhs_in = pltpu.make_async_copy(rhs_hbm, rhs, loc_sem.at[1])
    fac_in.start()
    rhs_in.start()

    barrier = pltpu.get_barrier_semaphore()

    def greet_row(p):
        @pl.when(p != r)
        def _():
            pl.semaphore_signal(barrier, inc=1, device_id=(p, c), device_id_type=MESH)

    def greet_z(d):
        pl.semaphore_signal(barrier, inc=1, device_id=(r, 2 * zpeer(d) + core), device_id_type=MESH)

    loop(0, NR, greet_row)
    loop(1, NZ, greet_z)
    pl.semaphore_signal(barrier, inc=1, device_id=mate, device_id_type=MESH)

    rhs_in.wait()
    fac_in.wait()

    def compact(i):
        for q in range(2):
            own[q, i] = fac[pl.ds(i * 512 + q, 256, stride=2), :].reshape(16, 16, KB)

    loop(0, NZ, compact)
    py[...] = jnp.zeros_like(py)
    pl.semaphore_wait(barrier, NR - 1 + NZ - 1 + 1)

    def cols(p):
        return pl.ds(pl.multiple_of(p * KB, KB), KB)

    def slice_of(which, p, h):
        if which == 2:
            return own.at[1, pl.ds(4 * h, 4), p]
        return own.at[0, p // 2, pl.ds(p % 2 * 8 + 4 * h, 4)]

    def half(q, k, h):
        return w.at[q, k, pl.ds(4 * h, 4)]

    def sc_rhs(panel, p):
        dst = xs.at[0, p] if panel == 0 else r1
        return remote(rhs.at[:, cols(p)], dst, s_rhs.at[p], r_rhs.at[panel], (p, c))

    def source(which):
        return 0 if which == 0 else 1

    def far(which, p):
        return jnp.logical_and(p // NX == 2, p % NX != source(which))

    def sc_fac(which, p, h):
        return remote(slice_of(which, p, h), half(which, c, h), s_sc.at[which, h, p], r_sc.at[which, h], (p, c))

    def sc_far(which, p, h):
        to = rel.at[which, pl.ds(4 * h, 4)]
        return remote(slice_of(which, p, h), to, s_sc.at[which, h, p], r_rel.at[which, h], (p % NX, c))

    def relay(which, h):
        got = rel.at[which, pl.ds(4 * h, 4)]
        return remote(got, half(which, c, h), s_rel.at[which, h], r_sc.at[which, h], ((r + 2 * NX) % NR, c))

    def sc_fac_go(which, h, act):
        def step(d):
            p = rowpeer(d)
            f = far(which, p)

            @pl.when(f)
            def _():
                act(sc_far(which, p, h))

            @pl.when(jnp.logical_not(f))
            def _():
                act(sc_fac(which, p, h))

        loop(1, NR, step)

    def sc_fac_start(which):
        for h in range(2):
            sc_fac_go(which, h, lambda cp: cp.start())

    def sc_fac_left(which):
        for h in range(2):
            sc_fac_go(which, h, lambda cp: cp.wait_send())

    def is_relay(which):
        return jnp.logical_and(r < NX, r != source(which))

    def relay_go(which, h):
        @pl.when(is_relay(which))
        def _():
            got = rel.at[which, pl.ds(4 * h, 4)]
            remote(got, got, s_rel.at[which, h], r_rel.at[which, h], (rowpeer(1), c)).wait_recv()
            relay(which, h).start()

    def rhs_start(panel):
        @pl.when(r == panel)
        def _():
            loop(1, NR, lambda d: sc_rhs(panel, rowpeer(d)).start())

    def last_start():
        @pl.when(r == 1)
        def _():
            sc_fac_start(2)

    @pl.when(r == 0)
    def _():
        sc_fac_start(0)
        xs[0, 0] = rhs[:, 0:KB]
        w[0, c] = own[0, 0, 0:8]

    @pl.when(r == 1)
    def _():
        sc_fac_start(1)
        r1[...] = rhs[:, KB : 2 * KB]
        w[1, c] = own[0, 0, 8:16]
        w[2, c] = own[1, :, 1]

    def swap(q):
        return remote(own.at[q], other.at[q], s_l.at[q], r_l.at[q], mate)

    for q in range(2):
        swap(q).start()

    def convert(src, lane):
        def step(i):
            at = pl.ds(pl.multiple_of(i * 256, 256), 256)
            for q in range(2):
                hi, lo = split(src[q, i].reshape(256, KB))
                lhi[q, at, cols(lane)] = hi
                llo[q, at, cols(lane)] = lo

        loop(0, NZ, step)

    def ag(b, d):
        return remote(xs.at[b, r], xs.at[b, r], s_ag.at[b, d], r_ag.at[b, r], (rowpeer(d), c))

    def ag_in(b, d):
        p = rowpeer(d)
        return remote(xs.at[b, p], xs.at[b, p], s_ag.at[b, d], r_ag.at[b, p], (p, c))

    def ag_start(b):
        loop(1, NR, lambda d: ag(b, d).start())

    def ag_wait(b):
        loop(1, NR, lambda d: ag_in(b, d).wait_recv())

    def zcopy(q, h, i, far_z, d):
        k = 2 * far_z + core
        return remote(half(q, k, h), half(q, k, h), s_z.at[q, h, i], r_z.at[q, h, far_z], (r, 2 * zpeer(d) + core))

    def zfirst(q, h):
        return [zcopy(q, h, i, z, d) for i, d in enumerate((2, NZ - 2, 1, NZ - 1))]

    def zsecond(q, h):
        left, right = zpeer(NZ - 2), zpeer(2)
        last = zcopy(q, h, 6, left, 2) if h == 0 else zcopy(q, h, 6, right, NZ - 2)
        return [last, zcopy(q, h, 4, left, 1), zcopy(q, h, 5, right, NZ - 1)]

    def zin(q, h, d):
        zcopy(q, h, 0, zpeer(d), 1).wait_recv()

    def xsend(q, d):
        k = 2 * zpeer(d) + core
        return remote(w.at[q, k], w.at[q, k], s_cx.at[q, d], r_cx.at[q, zpeer(d)], mate)

    def xrecv(q, d):
        k = 2 * zpeer(d) + 1 - core
        return remote(w.at[q, k], w.at[q, k], s_cx.at[q, d], r_cx.at[q, zpeer(d)], mate)

    def ready(q, k):
        hi, lo = split(w[q, k].reshape(KB, KB))
        at = cols(k)
        wb[q, 0:KB, at] = hi
        wb[q, KB : 2 * KB, at] = lo

    def slice_in(q, h):
        @pl.when(r != source(q))
        def _():
            remote(half(q, c, h), half(q, c, h), s_rhs.at[0], r_sc.at[q, h], (rowpeer(1), c)).wait_recv()

    def fetch(q):
        for h in range(2):
            relay_go(q, h)
            slice_in(q, h)
            for cp in zfirst(q, h):
                cp.start()
        xsend(q, 0).start()
        ready(q, c)

    def hand_on(q, h):
        zin(q, h, 2)
        zin(q, h, NZ - 2)
        for cp in zsecond(q, h):
            cp.start()

    def near(q):
        for d in (2, NZ - 2):
            xsend(q, d).start()
            ready(q, 2 * zpeer(d) + core)
        arrive(q, (1, NZ - 1))

    def arrive(q, which):
        for d in which:
            for h in range(2):
                zin(q, h, d)
            xsend(q, d).start()
            ready(q, 2 * zpeer(d) + core)

    def collect(q):
        def step(d):
            xrecv(q, d).wait_recv()
            ready(q, 2 * zpeer(d) + 1 - core)

        loop(0, NZ, step)

    def load_x(b):
        def step(k):
            hi, lo = split(xs[b, k])
            xb[0:MB, cols(k)] = hi
            xb[MB : 2 * MB, cols(k)] = lo

        loop(0, NR, step)

    def product(q):
        o = dot_nt(xb[...], wb[q])
        return o[0:MB, 0:KB] + o[MB : 2 * MB, 0:KB] + o[0:MB, KB : 2 * KB]

    def rhs0_in():
        @pl.when(r != 0)
        def _():
            remote(xs.at[0, r], xs.at[0, r], s_rhs.at[0], r_rhs.at[0], (rowpeer(1), c)).wait_recv()

    def rhs1_in():
        @pl.when(r != 1)
        def _():
            remote(r1, r1, s_rhs.at[0], r_rhs.at[1], (rowpeer(1), c)).wait_recv()

    def swap_in():
        for q in range(2):
            swap(q).wait_recv()

    def zorder(i):
        h = (i + 1) // 2
        return h + (i + 1) % 2 * (NZ - 2 * h)

    def a2a(d):
        p = zpeer(d)
        return remote(xs.at[1, pl.ds(2 * p, 2)], t.at[z], s_a.at[0, d], r_a.at[0, z], (r, 2 * p + core))

    def a2a_from(p):
        d = 1
        return remote(t.at[p], t.at[p], s_a.at[0, d], r_a.at[0, p], (r, 2 * p + core))

    def regroup(d):
        p = zpeer(d)
        return remote(py.at[p], pz.at[z], s_a.at[1, d], r_a.at[1, z], (r, 2 * p + core))

    def regroup_in(d):
        p = zpeer(d)
        return remote(pz.at[p], pz.at[p], s_a.at[1, d], r_a.at[1, p], (r, 2 * p + core))

    def spread(g, d):
        return remote(gx.at[g, r], gx.at[g, r], s_g.at[g, d], r_g.at[g, r], (rowpeer(d), c))

    def spread_in(g, d):
        p = rowpeer(d)
        return remote(gx.at[g, p], gx.at[g, p], s_g.at[g, d], r_g.at[g, p], (p, c))

    def to_owner():
        return remote(py, s1t.at[:, r], s_o, r_o.at[r], (1, c))

    def from_peer(d):
        p = rowpeer(d)
        return remote(py, s1t.at[:, p], s_o, r_o.at[p], (p, c))

    def dest(way, s):
        return (z + NZ - 1 - s) % NZ if way == 0 else (z + 1 + s) % NZ

    def hop(way, s, j):
        lanes = pl.ds(way * HALF + j * PIECE, PIECE)
        to = (z + 1) % NZ if way == 0 else (z + NZ - 1) % NZ
        return remote(
            acc.at[dest(way, s), :, lanes], slots.at[way, s, j], s_rs.at[way, s, j], r_rs.at[way, s, j],
            (r, 2 * to + core),
        )

    def left_scatter():
        @pl.when(r == 0)
        def _():
            loop(1, NR, lambda d: sc_rhs(0, rowpeer(d)).wait_send())
            sc_fac_left(0)

        @pl.when(r == 1)
        def _():
            loop(1, NR, lambda d: sc_rhs(1, rowpeer(d)).wait_send())
            sc_fac_left(1)
            sc_fac_left(2)

        for which in range(3):

            @pl.when(is_relay(which))
            def _(which=which):
                for h in range(2):
                    relay(which, h).wait_send()

    def left_swap():
        for q in range(2):
            swap(q).wait_send()

    def left_f(q):
        for h in range(2):
            for cp in zfirst(q, h) + zsecond(q, h):
                cp.wait_send()
        loop(0, NZ, lambda d: xsend(q, d).wait_send())

    def left_ag(b):
        loop(1, NR, lambda d: ag(b, d).wait_send())

    def left_a2a():
        loop(1, NZ, lambda d: a2a(d).wait_send())

    def left_regroup():
        loop(1, NZ, lambda d: regroup(d).wait_send())

    def left_spread():
        loop(1, NR, lambda d: spread(1, d).wait_send())

    def drain(s):
        for way in range(2):
            for j in range(SUB):
                hop(way, s, j).wait_send()

    convert(own, core)
    fetch(0)
    rhs_start(0)
    fetch(1)
    last_start()
    rhs_start(1)
    hand_on(0, 0)
    hand_on(0, 1)
    rhs0_in()
    ag_start(0)
    near(0)
    hand_on(1, 0)
    hand_on(1, 1)
    arrive(0, (3, NZ - 3, 4))
    near(1)
    fetch(2)
    ag_wait(0)
    load_x(0)
    collect(0)
    xs[1, r] = product(0)
    ag_start(1)
    hand_on(2, 0)
    hand_on(2, 1)
    arrive(1, (3, NZ - 3, 4))
    swap_in()
    convert(other, 1 - core)
    near(2)
    arrive(2, (3, NZ - 3, 4))
    ag_wait(1)
    load_x(1)
    collect(1)
    rhs1_in()
    xs[2, r] = r1[...] - product(1)
    ag_start(2)
    loop(1, NZ, lambda d: a2a(d).start())
    t[z] = xs[1, pl.ds(2 * z, 2)]
    left_swap()
    for q in range(2):
        left_f(q)
        left_ag(q)
    ag_wait(2)
    collect(2)
    load_x(2)
    turned = dot_nt(wb[2], xb[0:MB, :])
    turned = turned[0:KB] + turned[KB : 2 * KB] + dot_nt(wb[2, 0:KB, :], xb[MB : 2 * MB, :])
    py[:, :, 0:MB] = turned.reshape(NZ, 16, MB)
    loop(1, NZ, lambda d: regroup(d).start())
    pz[z] = py[z]

    left_f(2)
    left_ag(2)
    loop(1, NZ, lambda d: regroup_in(d).wait_recv())

    def pair(g):
        return (z + NZ - 1 - g) % NZ, z if g == 3 else (z + 1 + g) % NZ

    def spread_start(g):
        for i in range(2):
            one, two = pair(2 * g + i)
            gx[g, r, i] = pz[one] + pltpu.roll(pz[two], MB, 1)
        loop(1, NR, lambda d: spread(g, d).start())

    def spread_end(g):
        loop(1, NR, lambda d: spread_in(g, d).wait_recv())
        for n in range(2):
            for k in range(2):
                hi, lo = split(gx[g, 8 * k : 8 * k + 8, n].reshape(KB, KB).T)
                for i, d in enumerate(pair(2 * g + n)):
                    rows = pl.ds(pl.multiple_of(d * MB, MB), MB)
                    tb[0, rows, k * KB : (k + 1) * KB] = hi[i * MB : (i + 1) * MB]
                    tb[1, rows, k * KB : (k + 1) * KB] = lo[i * MB : (i + 1) * MB]

    spread_start(0)

    def first_in(d, away):
        if away:
            a2a_from(d).wait_recv()
        rows = pl.ds(pl.multiple_of(d * MB, MB), MB)
        for k in range(2):
            hi, lo = split(t[d, k])
            ta[0, rows, k * KB : (k + 1) * KB] = hi
            ta[1, rows, k * KB : (k + 1) * KB] = lo

    def first_in_step(s):
        first_in(dest(0, s), True)
        first_in(z if s == 3 else dest(1, s), s != 3)

    def part(q, way, s):
        d = dest(way, s)
        rows = pl.ds(pl.multiple_of(d * MB, MB), MB)
        from_ = ta if q == 0 else tb
        hi, lo = from_[0, rows, :], from_[1, rows, :]
        for j in range(HALF // 512):
            at = slice(way * HALF + j * 512, way * HALF + (j + 1) * 512)
            o = dot_nt(jnp.concatenate([hi, lo], axis=0), lhi[q, at, :])
            o = o[0:MB] + o[MB : 2 * MB] + dot_nt(hi, llo[q, at, :])
            if q == 0:
                acc[d, :, at] = o
            else:
                acc[d, :, at] += o

    def parts(q, s):
        for way in range(2):
            part(q, way, s)

    def pass_on(way, s, j):
        if not (isinstance(s, int) and s == NZ - 1):
            hop(way, s, j).start()

    def ring(s):
        if isinstance(s, int) and s == 1:
            spread_end(1)
            parts(1, 2)
        for j in range(SUB):
            for way in range(2):
                lanes = slice(way * HALF + j * PIECE, way * HALF + (j + 1) * PIECE)
                hop(way, s, j).wait_recv()
                acc[dest(way, s + 1), :, lanes] += slots[way, s, j]
                pass_on(way, s + 1, j)
            if j == 1 and not (isinstance(s, int) and s == 0):
                drain(s - 1)
            if isinstance(s, int) and s == 6:
                continue
            if j == 0:
                if isinstance(s, int) and s < 2:
                    first_in_step(s + 2)
                parts(0, s + 2)
            if j == SUB - 1:
                if isinstance(s, int) and s == 0:
                    continue
                parts(1, s + 2)

    for s in range(2):
        first_in_step(s)
        parts(0, s)
    loop(1, NR, lambda d: spread(0, d).wait_send())
    spread_start(1)
    spread_end(0)

    def left_late():
        left_a2a()
        left_regroup()
        left_spread()

    @pl.when(r > 1)
    def _():
        for way in range(2):
            part(1, way, 0)
            for j in range(SUB):
                hop(way, 0, j).start()
        parts(1, 1)
        left_late()
        ring(0)
        ring(1)
        to_owner().start()
        loop(2, NZ - 2, ring)
        ring(NZ - 2)
        out_ref[...] = rhs[...] - acc[z]
        to_owner().wait_send()
        drain(NZ - 2)

    def no_ring():
        spread_end(1)
        first_in_step(2)
        first_in_step(3)
        left_late()

    @pl.when(r == 0)
    def _():
        no_ring()
        to_owner().start()
        for k in range(NR):
            out_ref[:, k * KB : (k + 1) * KB] = xs[1, k]
        to_owner().wait_send()

    @pl.when(r == 1)
    def _():
        no_ring()
        s1t[:, 1] = py[...]
        loop(1, NR, lambda d: from_peer(d).wait_recv())
        for k in range(NR):
            block = s1t[k // 2, k % 2 * 8 : k % 2 * 8 + 8].reshape(KB, KB)
            out_ref[:, k * KB : (k + 1) * KB] = block.T[0:MB]

    left_scatter()


def local(right_side, factor):
    rows = factor.shape[0]
    dma = pltpu.SemaphoreType.DMA
    return pl.pallas_call(
        kernel,
        name="panels",
        out_shape=jax.ShapeDtypeStruct((MB, NB), F32),
        in_specs=[pl.BlockSpec(memory_space=pl.ANY)] * 2,
        out_specs=pl.BlockSpec(memory_space=pltpu.VMEM),
        scratch_shapes=[
            pltpu.VMEM((2 * NB, KB), F32),
            pltpu.VMEM((MB, NB), F32),
            pltpu.VMEM((2, NZ, 16, 16, KB), F32),
            pltpu.VMEM((2, NZ, 16, 16, KB), F32),
            pltpu.VMEM((2, NB, 2 * KB), BF16),
            pltpu.VMEM((2, NB, 2 * KB), BF16),
            pltpu.VMEM((3, 16, 8, 16, KB), F32),
            pltpu.VMEM((3, 8, 16, KB), F32),
            pltpu.VMEM((3, 2 * KB, NB), BF16),
            pltpu.VMEM((3, NR, MB, KB), F32),
            pltpu.VMEM((MB, KB), F32),
            pltpu.VMEM((2 * MB, NB), BF16),
            pltpu.VMEM((NZ, 2, MB, KB), F32),
            pltpu.VMEM((NZ, 16, KB), F32),
            pltpu.VMEM((NZ, 16, KB), F32),
            pltpu.VMEM((2, NR, 2, 16, KB), F32),
            pltpu.VMEM((NZ, NR, 16, KB), F32),
            pltpu.VMEM((2, MC, 2 * KB), BF16),
            pltpu.VMEM((2, MC, 2 * KB), BF16),
            pltpu.VMEM((NZ, MB, NB), F32),
            pltpu.VMEM((2, NZ - 1, SUB, MB, PIECE), F32),
            dma((2,)),
            dma((NR,)),
            dma((2,)),
            dma((3, 2, NR)),
            dma((3, 2)),
            dma((3, 2)),
            dma((3, 2)),
            dma((3, 2, 7)),
            dma((3, 2, NZ)),
            dma((3, NZ)),
            dma((3, NZ)),
            dma((3, NR)),
            dma((3, NR)),
            dma((2, NZ)),
            dma((2, NZ)),
            dma((2, NR)),
            dma((2, NR)),
            dma,
            dma((NR,)),
            dma((2,)),
            dma((2,)),
            dma((2, NZ - 1, SUB)),
            dma((2, NZ - 1, SUB)),
        ],
        compiler_params=pltpu.CompilerParams(
            collective_id=0, has_side_effects=True, vmem_limit_bytes=60 * 2**20
        ),
    )(right_side, factor.reshape(2 * rows, KB))


def solution(mesh):
    in_specs = (P("col", "row"), P("row", None, "col"))
    out_specs = P("col", "row")
    return jax.shard_map(local, mesh=mesh, in_specs=in_specs, out_specs=out_specs, check_vma=False)
```

```python
import jax
import jax.numpy as jnp
from jax import lax
from jax.experimental import pallas as pl
from jax.experimental.pallas import tpu as pltpu
from jax.sharding import PartitionSpec as P

STOP = 99
MESH = pl.DeviceIdType.MESH
F32, BF16 = jnp.float32, jnp.bfloat16
NR = 16
NX = 4
NZ = 8
NB = 2048
MB = 48
KB = 128
MC = NZ * MB
SUB = 4
HALF = NB // 2
PIECE = HALF // SUB


def split(x):
    hi = x.astype(BF16)
    return hi, (x - hi.astype(F32)).astype(BF16)


def dot_nt(a, b):
    return lax.dot_general(a, b, (((1,), (1,)), ((), ())), preferred_element_type=F32)


def remote(src, dst, ssem, rsem, dev):
    return pltpu.make_async_remote_copy(
        src_ref=src, dst_ref=dst, send_sem=ssem, recv_sem=rsem, device_id=dev, device_id_type=MESH
    )


def loop(lo, hi, body):
    def step(i, carry):
        body(i)
        return carry

    lax.fori_loop(lo, hi, step, 0)


def kernel(
    rhs_hbm, fac_hbm, out_ref,
    fac, rhs, own, other, lhi, llo, w, rel, wb, xs, r1, xb, t, py, pz, gx, s1t, ta, tb, acc, slots,
    loc_sem, s_rhs, r_rhs, s_sc, r_sc, s_rel, r_rel, s_z, r_z, s_cx, r_cx, s_ag, r_ag, s_a, r_a, s_g, r_g, s_o, r_o,
    s_l, r_l, s_rs, r_rs,
):
    r = lax.axis_index("row")
    c = lax.axis_index("col")
    z = c // 2
    core = c % 2
    mate = (r, c + 1 - 2 * core)

    def rowpeer(d):
        return (r + d * (3 + 10 * core)) % NR

    def zpeer(d):
        return (z + d) % NZ

    fac_in = pltpu.make_async_copy(fac_hbm, fac, loc_sem.at[0])
    rhs_in = pltpu.make_async_copy(rhs_hbm, rhs, loc_sem.at[1])
    fac_in.start()
    rhs_in.start()

    barrier = pltpu.get_barrier_semaphore()

    def greet_row(p):
        @pl.when(p != r)
        def _():
            pl.semaphore_signal(barrier, inc=1, device_id=(p, c), device_id_type=MESH)

    def greet_z(d):
        pl.semaphore_signal(barrier, inc=1, device_id=(r, 2 * zpeer(d) + core), device_id_type=MESH)

    loop(0, NR, greet_row)
    loop(1, NZ, greet_z)
    pl.semaphore_signal(barrier, inc=1, device_id=mate, device_id_type=MESH)

    rhs_in.wait()
    fac_in.wait()

    def compact(i):
        for q in range(2):
            own[q, i] = fac[pl.ds(i * 512 + q, 256, stride=2), :].reshape(16, 16, KB)

    loop(0, NZ, compact)
    py[...] = jnp.zeros_like(py)
    pl.semaphore_wait(barrier, NR - 1 + NZ - 1 + 1)

    def cols(p):
        return pl.ds(pl.multiple_of(p * KB, KB), KB)

    def slice_of(which, p, h):
        if which == 2:
            return own.at[1, pl.ds(4 * h, 4), p]
        return own.at[0, p // 2, pl.ds(p % 2 * 8 + 4 * h, 4)]

    def half(q, k, h):
        return w.at[q, k, pl.ds(4 * h, 4)]

    def sc_rhs(panel, p):
        dst = xs.at[0, p] if panel == 0 else r1
        return remote(rhs.at[:, cols(p)], dst, s_rhs.at[p], r_rhs.at[panel], (p, c))

    def source(which):
        return 0 if which == 0 else 1

    def far(which, p):
        return jnp.logical_and(p // NX == 2, p % NX != source(which))

    def sc_fac(which, p, h):
        return remote(slice_of(which, p, h), half(which, c, h), s_sc.at[which, h, p], r_sc.at[which, h], (p, c))

    def sc_far(which, p, h):
        to = rel.at[which, pl.ds(4 * h, 4)]
        return remote(slice_of(which, p, h), to, s_sc.at[which, h, p], r_rel.at[which, h], (p % NX, c))

    def relay(which, h):
        got = rel.at[which, pl.ds(4 * h, 4)]
        return remote(got, half(which, c, h), s_rel.at[which, h], r_sc.at[which, h], ((r + 2 * NX) % NR, c))

    def sc_fac_go(which, h, act):
        def step(d):
            p = rowpeer(d)
            f = far(which, p)

            @pl.when(f)
            def _():
                act(sc_far(which, p, h))

            @pl.when(jnp.logical_not(f))
            def _():
                act(sc_fac(which, p, h))

        loop(1, NR, step)

    def sc_fac_start(which):
        for h in range(2):
            sc_fac_go(which, h, lambda cp: cp.start())

    def sc_fac_left(which):
        for h in range(2):
            sc_fac_go(which, h, lambda cp: cp.wait_send())

    def is_relay(which):
        return jnp.logical_and(r < NX, r != source(which))

    def relay_go(which, h):
        @pl.when(is_relay(which))
        def _():
            got = rel.at[which, pl.ds(4 * h, 4)]
            remote(got, got, s_rel.at[which, h], r_rel.at[which, h], (rowpeer(1), c)).wait_recv()
            relay(which, h).start()

    def rhs_start(panel):
        @pl.when(r == panel)
        def _():
            loop(1, NR, lambda d: sc_rhs(panel, rowpeer(d)).start())

    def last_start():
        @pl.when(r == 1)
        def _():
            sc_fac_start(2)

    @pl.when(r == 0)
    def _():
        sc_fac_start(0)
        xs[0, 0] = rhs[:, 0:KB]
        w[0, c] = own[0, 0, 0:8]

    @pl.when(r == 1)
    def _():
        sc_fac_start(1)
        r1[...] = rhs[:, KB : 2 * KB]
        w[1, c] = own[0, 0, 8:16]
        w[2, c] = own[1, :, 1]

    def swap(q):
        return remote(own.at[q], other.at[q], s_l.at[q], r_l.at[q], mate)

    for q in range(2):
        swap(q).start()

    def convert(src, lane):
        def step(i):
            at = pl.ds(pl.multiple_of(i * 256, 256), 256)
            for q in range(2):
                hi, lo = split(src[q, i].reshape(256, KB))
                lhi[q, at, cols(lane)] = hi
                llo[q, at, cols(lane)] = lo

        loop(0, NZ, step)

    def ag(b, d):
        return remote(xs.at[b, r], xs.at[b, r], s_ag.at[b, d], r_ag.at[b, r], (rowpeer(d), c))

    def ag_in(b, d):
        p = rowpeer(d)
        return remote(xs.at[b, p], xs.at[b, p], s_ag.at[b, d], r_ag.at[b, p], (p, c))

    def ag_start(b):
        loop(1, NR, lambda d: ag(b, d).start())

    def ag_wait(b):
        loop(1, NR, lambda d: ag_in(b, d).wait_recv())

    def zcopy(q, h, i, far_z, d):
        k = 2 * far_z + core
        return remote(half(q, k, h), half(q, k, h), s_z.at[q, h, i], r_z.at[q, h, far_z], (r, 2 * zpeer(d) + core))

    def zfirst(q, h):
        return [zcopy(q, h, i, z, d) for i, d in enumerate((2, NZ - 2, 1, NZ - 1))]

    def zsecond(q, h):
        left, right = zpeer(NZ - 2), zpeer(2)
        last = zcopy(q, h, 6, left, 2) if h == 0 else zcopy(q, h, 6, right, NZ - 2)
        return [last, zcopy(q, h, 4, left, 1), zcopy(q, h, 5, right, NZ - 1)]

    def zin(q, h, d):
        zcopy(q, h, 0, zpeer(d), 1).wait_recv()

    def xsend(q, d):
        k = 2 * zpeer(d) + core
        return remote(w.at[q, k], w.at[q, k], s_cx.at[q, d], r_cx.at[q, zpeer(d)], mate)

    def xrecv(q, d):
        k = 2 * zpeer(d) + 1 - core
        return remote(w.at[q, k], w.at[q, k], s_cx.at[q, d], r_cx.at[q, zpeer(d)], mate)

    def ready(q, k):
        hi, lo = split(w[q, k].reshape(KB, KB))
        at = cols(k)
        wb[q, 0:KB, at] = hi
        wb[q, KB : 2 * KB, at] = lo

    def slice_in(q, h):
        @pl.when(r != source(q))
        def _():
            remote(half(q, c, h), half(q, c, h), s_rhs.at[0], r_sc.at[q, h], (rowpeer(1), c)).wait_recv()

    def fetch(q):
        for h in range(2):
            relay_go(q, h)
            slice_in(q, h)
            for cp in zfirst(q, h):
                cp.start()
        xsend(q, 0).start()
        ready(q, c)

    def hand_on(q, h):
        zin(q, h, 2)
        zin(q, h, NZ - 2)
        for cp in zsecond(q, h):
            cp.start()

    def near(q):
        for d in (2, NZ - 2):
            xsend(q, d).start()
            ready(q, 2 * zpeer(d) + core)
        arrive(q, (1, NZ - 1))

    def arrive(q, which):
        for d in which:
            for h in range(2):
                zin(q, h, d)
            xsend(q, d).start()
            ready(q, 2 * zpeer(d) + core)

    def collect(q):
        def step(d):
            xrecv(q, d).wait_recv()
            ready(q, 2 * zpeer(d) + 1 - core)

        loop(0, NZ, step)

    def load_x(b):
        def step(k):
            hi, lo = split(xs[b, k])
            xb[0:MB, cols(k)] = hi
            xb[MB : 2 * MB, cols(k)] = lo

        loop(0, NR, step)

    def product(q):
        o = dot_nt(xb[...], wb[q])
        return o[0:MB, 0:KB] + o[MB : 2 * MB, 0:KB] + o[0:MB, KB : 2 * KB]

    def rhs0_in():
        @pl.when(r != 0)
        def _():
            remote(xs.at[0, r], xs.at[0, r], s_rhs.at[0], r_rhs.at[0], (rowpeer(1), c)).wait_recv()

    def rhs1_in():
        @pl.when(r != 1)
        def _():
            remote(r1, r1, s_rhs.at[0], r_rhs.at[1], (rowpeer(1), c)).wait_recv()

    def swap_in():
        for q in range(2):
            swap(q).wait_recv()

    def zorder(i):
        h = (i + 1) // 2
        return h + (i + 1) % 2 * (NZ - 2 * h)

    def a2a(d):
        p = zpeer(d)
        return remote(xs.at[1, pl.ds(2 * p, 2)], t.at[z], s_a.at[0, d], r_a.at[0, z], (r, 2 * p + core))

    def a2a_from(p):
        d = 1
        return remote(t.at[p], t.at[p], s_a.at[0, d], r_a.at[0, p], (r, 2 * p + core))

    def regroup(d):
        p = zpeer(d)
        return remote(py.at[p], pz.at[z], s_a.at[1, d], r_a.at[1, z], (r, 2 * p + core))

    def regroup_in(d):
        p = zpeer(d)
        return remote(pz.at[p], pz.at[p], s_a.at[1, d], r_a.at[1, p], (r, 2 * p + core))

    def spread(g, d):
        return remote(gx.at[g, r], gx.at[g, r], s_g.at[g, d], r_g.at[g, r], (rowpeer(d), c))

    def spread_in(g, d):
        p = rowpeer(d)
        return remote(gx.at[g, p], gx.at[g, p], s_g.at[g, d], r_g.at[g, p], (p, c))

    def to_owner():
        return remote(py, s1t.at[:, r], s_o, r_o.at[r], (1, c))

    def from_peer(d):
        p = rowpeer(d)
        return remote(py, s1t.at[:, p], s_o, r_o.at[p], (p, c))

    def dest(way, s):
        return (z + NZ - 1 - s) % NZ if way == 0 else (z + 1 + s) % NZ

    def hop(way, s, j):
        lanes = pl.ds(way * HALF + j * PIECE, PIECE)
        to = (z + 1) % NZ if way == 0 else (z + NZ - 1) % NZ
        return remote(
            acc.at[dest(way, s), :, lanes], slots.at[way, s, j], s_rs.at[way, s, j], r_rs.at[way, s, j],
            (r, 2 * to + core),
        )

    def left_scatter():
        @pl.when(r == 0)
        def _():
            loop(1, NR, lambda d: sc_rhs(0, rowpeer(d)).wait_send())
            sc_fac_left(0)

        @pl.when(r == 1)
        def _():
            loop(1, NR, lambda d: sc_rhs(1, rowpeer(d)).wait_send())
            sc_fac_left(1)
            sc_fac_left(2)

        for which in range(3):

            @pl.when(is_relay(which))
            def _(which=which):
                for h in range(2):
                    relay(which, h).wait_send()

    def left_swap():
        for q in range(2):
            swap(q).wait_send()

    def left_f(q):
        for h in range(2):
            for cp in zfirst(q, h) + zsecond(q, h):
                cp.wait_send()
        loop(0, NZ, lambda d: xsend(q, d).wait_send())

    def left_ag(b):
        loop(1, NR, lambda d: ag(b, d).wait_send())

    def left_a2a():
        loop(1, NZ, lambda d: a2a(d).wait_send())

    def left_regroup():
        loop(1, NZ, lambda d: regroup(d).wait_send())

    def left_spread():
        loop(1, NR, lambda d: spread(1, d).wait_send())

    def drain(s):
        for way in range(2):
            for j in range(SUB):
                hop(way, s, j).wait_send()

    convert(own, core)
    fetch(0)
    rhs_start(0)
    fetch(1)
    last_start()
    rhs_start(1)
    hand_on(0, 0)
    hand_on(0, 1)
    rhs0_in()
    ag_start(0)
    near(0)
    hand_on(1, 0)
    hand_on(1, 1)
    arrive(0, (3, NZ - 3, 4))
    near(1)
    fetch(2)
    ag_wait(0)
    load_x(0)
    collect(0)
    xs[1, r] = product(0)
    ag_start(1)
    hand_on(2, 0)
    hand_on(2, 1)
    arrive(1, (3, NZ - 3, 4))
    near(2)
    arrive(2, (3, NZ - 3, 4))
    ag_wait(1)
    load_x(1)
    collect(1)
    rhs1_in()
    xs[2, r] = r1[...] - product(1)
    ag_start(2)
    loop(1, NZ, lambda d: a2a(d).start())
    t[z] = xs[1, pl.ds(2 * z, 2)]
    swap_in()
    convert(other, 1 - core)
    left_swap()
    for q in range(2):
        left_f(q)
        left_ag(q)
    ag_wait(2)
    collect(2)
    load_x(2)
    turned = dot_nt(wb[2], xb[0:MB, :])
    turned = turned[0:KB] + turned[KB : 2 * KB] + dot_nt(wb[2, 0:KB, :], xb[MB : 2 * MB, :])
    py[:, :, 0:MB] = turned.reshape(NZ, 16, MB)
    loop(1, NZ, lambda d: regroup(d).start())
    pz[z] = py[z]

    left_f(2)
    left_ag(2)
    loop(1, NZ, lambda d: regroup_in(d).wait_recv())

    def pair(g):
        return (z + NZ - 1 - g) % NZ, z if g == 3 else (z + 1 + g) % NZ

    def spread_start(g):
        for i in range(2):
            one, two = pair(2 * g + i)
            gx[g, r, i] = pz[one] + pltpu.roll(pz[two], MB, 1)
        loop(1, NR, lambda d: spread(g, d).start())

    def spread_end(g):
        loop(1, NR, lambda d: spread_in(g, d).wait_recv())
        for n in range(2):
            for k in range(2):
                hi, lo = split(gx[g, 8 * k : 8 * k + 8, n].reshape(KB, KB).T)
                for i, d in enumerate(pair(2 * g + n)):
                    rows = pl.ds(pl.multiple_of(d * MB, MB), MB)
                    tb[0, rows, k * KB : (k + 1) * KB] = hi[i * MB : (i + 1) * MB]
                    tb[1, rows, k * KB : (k + 1) * KB] = lo[i * MB : (i + 1) * MB]

    spread_start(0)

    def first_in(d, away):
        if away:
            a2a_from(d).wait_recv()
        rows = pl.ds(pl.multiple_of(d * MB, MB), MB)
        for k in range(2):
            hi, lo = split(t[d, k])
            ta[0, rows, k * KB : (k + 1) * KB] = hi
            ta[1, rows, k * KB : (k + 1) * KB] = lo

    def first_in_step(s):
        first_in(dest(0, s), True)
        first_in(z if s == 3 else dest(1, s), s != 3)

    def part(q, way, s):
        d = dest(way, s)
        rows = pl.ds(pl.multiple_of(d * MB, MB), MB)
        from_ = ta if q == 0 else tb
        hi, lo = from_[0, rows, :], from_[1, rows, :]
        for j in range(HALF // 512):
            at = slice(way * HALF + j * 512, way * HALF + (j + 1) * 512)
            o = dot_nt(jnp.concatenate([hi, lo], axis=0), lhi[q, at, :])
            o = o[0:MB] + o[MB : 2 * MB] + dot_nt(hi, llo[q, at, :])
            if q == 0:
                acc[d, :, at] = o
            else:
                acc[d, :, at] += o

    def parts(q, s):
        for way in range(2):
            part(q, way, s)

    def pass_on(way, s, j):
        if not (isinstance(s, int) and s == NZ - 1):
            hop(way, s, j).start()

    def ring(s):
        if isinstance(s, int) and s == 1:
            spread_end(1)
            parts(1, 2)
        for j in range(SUB):
            for way in range(2):
                lanes = slice(way * HALF + j * PIECE, way * HALF + (j + 1) * PIECE)
                hop(way, s, j).wait_recv()
                acc[dest(way, s + 1), :, lanes] += slots[way, s, j]
                pass_on(way, s + 1, j)
            if j == 1 and not (isinstance(s, int) and s == 0):
                drain(s - 1)
            if isinstance(s, int) and s == 6:
                continue
            if j == 0:
                if isinstance(s, int) and s < 2:
                    first_in_step(s + 2)
                parts(0, s + 2)
            if j == SUB - 1:
                if isinstance(s, int) and s == 0:
                    continue
                parts(1, s + 2)

    for s in range(2):
        first_in_step(s)
        parts(0, s)
    loop(1, NR, lambda d: spread(0, d).wait_send())
    spread_start(1)
    spread_end(0)

    def left_late():
        left_a2a()
        left_regroup()
        left_spread()

    @pl.when(r > 1)
    def _():
        for way in range(2):
            part(1, way, 0)
            for j in range(SUB):
                hop(way, 0, j).start()
        parts(1, 1)
        left_late()
        ring(0)
        ring(1)
        to_owner().start()
        loop(2, NZ - 2, ring)
        ring(NZ - 2)
        out_ref[...] = rhs[...] - acc[z]
        to_owner().wait_send()
        drain(NZ - 2)

    def no_ring():
        spread_end(1)
        first_in_step(2)
        first_in_step(3)
        left_late()

    @pl.when(r == 0)
    def _():
        no_ring()
        to_owner().start()
        for k in range(NR):
            out_ref[:, k * KB : (k + 1) * KB] = xs[1, k]
        to_owner().wait_send()

    @pl.when(r == 1)
    def _():
        no_ring()
        s1t[:, 1] = py[...]
        loop(1, NR, lambda d: from_peer(d).wait_recv())
        for k in range(NR):
            block = s1t[k // 2, k % 2 * 8 : k % 2 * 8 + 8].reshape(KB, KB)
            out_ref[:, k * KB : (k + 1) * KB] = block.T[0:MB]

    left_scatter()


def local(right_side, factor):
    rows = factor.shape[0]
    dma = pltpu.SemaphoreType.DMA
    return pl.pallas_call(
        kernel,
        name="panels",
        out_shape=jax.ShapeDtypeStruct((MB, NB), F32),
        in_specs=[pl.BlockSpec(memory_space=pl.ANY)] * 2,
        out_specs=pl.BlockSpec(memory_space=pltpu.VMEM),
        scratch_shapes=[
            pltpu.VMEM((2 * NB, KB), F32),
            pltpu.VMEM((MB, NB), F32),
            pltpu.VMEM((2, NZ, 16, 16, KB), F32),
            pltpu.VMEM((2, NZ, 16, 16, KB), F32),
            pltpu.VMEM((2, NB, 2 * KB), BF16),
            pltpu.VMEM((2, NB, 2 * KB), BF16),
            pltpu.VMEM((3, 16, 8, 16, KB), F32),
            pltpu.VMEM((3, 8, 16, KB), F32),
            pltpu.VMEM((3, 2 * KB, NB), BF16),
            pltpu.VMEM((3, NR, MB, KB), F32),
            pltpu.VMEM((MB, KB), F32),
            pltpu.VMEM((2 * MB, NB), BF16),
            pltpu.VMEM((NZ, 2, MB, KB), F32),
            pltpu.VMEM((NZ, 16, KB), F32),
            pltpu.VMEM((NZ, 16, KB), F32),
            pltpu.VMEM((2, NR, 2, 16, KB), F32),
            pltpu.VMEM((NZ, NR, 16, KB), F32),
            pltpu.VMEM((2, MC, 2 * KB), BF16),
            pltpu.VMEM((2, MC, 2 * KB), BF16),
            pltpu.VMEM((NZ, MB, NB), F32),
            pltpu.VMEM((2, NZ - 1, SUB, MB, PIECE), F32),
            dma((2,)),
            dma((NR,)),
            dma((2,)),
            dma((3, 2, NR)),
            dma((3, 2)),
            dma((3, 2)),
            dma((3, 2)),
            dma((3, 2, 7)),
            dma((3, 2, NZ)),
            dma((3, NZ)),
            dma((3, NZ)),
            dma((3, NR)),
            dma((3, NR)),
            dma((2, NZ)),
            dma((2, NZ)),
            dma((2, NR)),
            dma((2, NR)),
            dma,
            dma((NR,)),
            dma((2,)),
            dma((2,)),
            dma((2, NZ - 1, SUB)),
            dma((2, NZ - 1, SUB)),
        ],
        compiler_params=pltpu.CompilerParams(
            collective_id=0, has_side_effects=True, vmem_limit_bytes=60 * 2**20
        ),
    )(right_side, factor.reshape(2 * rows, KB))


def solution(mesh):
    in_specs = (P("col", "row"), P("row", None, "col"))
    out_specs = P("col", "row")
    return jax.shard_map(local, mesh=mesh, in_specs=in_specs, out_specs=out_specs, check_vma=False)
```

```python
import jax
import jax.numpy as jnp
from jax import lax
from jax.experimental import pallas as pl
from jax.experimental.pallas import tpu as pltpu
from jax.sharding import PartitionSpec as P

STOP = 99
MESH = pl.DeviceIdType.MESH
F32, BF16 = jnp.float32, jnp.bfloat16
NR = 16
NX = 4
NZ = 8
NB = 2048
MB = 48
KB = 128
MC = NZ * MB
SUB = 4
HALF = NB // 2
PIECE = HALF // SUB


def split(x):
    hi = x.astype(BF16)
    return hi, (x - hi.astype(F32)).astype(BF16)


def dot_nt(a, b):
    return lax.dot_general(a, b, (((1,), (1,)), ((), ())), preferred_element_type=F32)


def remote(src, dst, ssem, rsem, dev):
    return pltpu.make_async_remote_copy(
        src_ref=src, dst_ref=dst, send_sem=ssem, recv_sem=rsem, device_id=dev, device_id_type=MESH
    )


def loop(lo, hi, body):
    def step(i, carry):
        body(i)
        return carry

    lax.fori_loop(lo, hi, step, 0)


def kernel(
    rhs_hbm, fac_hbm, out_ref,
    fac, rhs, own, other, lhi, llo, w, rel, wb, xs, r1, xb, t, py, pz, gx, s1t, ta, tb, acc, slots,
    loc_sem, s_rhs, r_rhs, s_sc, r_sc, s_rel, r_rel, s_z, r_z, s_cx, r_cx, s_ag, r_ag, s_a, r_a, s_g, r_g, s_o, r_o,
    s_l, r_l, s_rs, r_rs,
):
    r = lax.axis_index("row")
    c = lax.axis_index("col")
    z = c // 2
    core = c % 2
    mate = (r, c + 1 - 2 * core)

    def rowpeer(d):
        return (r + d * (3 + 10 * core)) % NR

    def zpeer(d):
        return (z + d) % NZ

    fac_in = pltpu.make_async_copy(fac_hbm, fac, loc_sem.at[0])
    rhs_in = pltpu.make_async_copy(rhs_hbm, rhs, loc_sem.at[1])
    fac_in.start()
    rhs_in.start()

    barrier = pltpu.get_barrier_semaphore()

    def greet_row(p):
        @pl.when(p != r)
        def _():
            pl.semaphore_signal(barrier, inc=1, device_id=(p, c), device_id_type=MESH)

    def greet_z(d):
        pl.semaphore_signal(barrier, inc=1, device_id=(r, 2 * zpeer(d) + core), device_id_type=MESH)

    loop(0, NR, greet_row)
    loop(1, NZ, greet_z)
    pl.semaphore_signal(barrier, inc=1, device_id=mate, device_id_type=MESH)

    rhs_in.wait()
    fac_in.wait()

    def compact(i):
        for q in range(2):
            own[q, i] = fac[pl.ds(i * 512 + q, 256, stride=2), :].reshape(16, 16, KB)

    loop(0, NZ, compact)
    py[...] = jnp.zeros_like(py)
    pl.semaphore_wait(barrier, NR - 1 + NZ - 1 + 1)

    def cols(p):
        return pl.ds(pl.multiple_of(p * KB, KB), KB)

    def slice_of(which, p, h):
        if which == 2:
            return own.at[1, pl.ds(4 * h, 4), p]
        return own.at[0, p // 2, pl.ds(p % 2 * 8 + 4 * h, 4)]

    def half(q, k, h):
        return w.at[q, k, pl.ds(4 * h, 4)]

    def sc_rhs(panel, p):
        dst = xs.at[0, p] if panel == 0 else r1
        return remote(rhs.at[:, cols(p)], dst, s_rhs.at[p], r_rhs.at[panel], (p, c))

    def source(which):
        return 0 if which == 0 else 1

    def far(which, p):
        return jnp.logical_and(p // NX == 2, p % NX != source(which))

    def sc_fac(which, p, h):
        return remote(slice_of(which, p, h), half(which, c, h), s_sc.at[which, h, p], r_sc.at[which, h], (p, c))

    def sc_far(which, p, h):
        to = rel.at[which, pl.ds(4 * h, 4)]
        return remote(slice_of(which, p, h), to, s_sc.at[which, h, p], r_rel.at[which, h], (p % NX, c))

    def relay(which, h):
        got = rel.at[which, pl.ds(4 * h, 4)]
        return remote(got, half(which, c, h), s_rel.at[which, h], r_sc.at[which, h], ((r + 2 * NX) % NR, c))

    def sc_fac_go(which, h, act):
        def step(d):
            p = rowpeer(d)
            f = far(which, p)

            @pl.when(f)
            def _():
                act(sc_far(which, p, h))

            @pl.when(jnp.logical_not(f))
            def _():
                act(sc_fac(which, p, h))

        loop(1, NR, step)

    def sc_fac_start(which):
        for h in range(2):
            sc_fac_go(which, h, lambda cp: cp.start())

    def sc_fac_left(which):
        for h in range(2):
            sc_fac_go(which, h, lambda cp: cp.wait_send())

    def is_relay(which):
        return jnp.logical_and(r < NX, r != source(which))

    def relay_go(which, h):
        @pl.when(is_relay(which))
        def _():
            got = rel.at[which, pl.ds(4 * h, 4)]
            remote(got, got, s_rel.at[which, h], r_rel.at[which, h], (rowpeer(1), c)).wait_recv()
            relay(which, h).start()

    def rhs_start(panel):
        @pl.when(r == panel)
        def _():
            loop(1, NR, lambda d: sc_rhs(panel, rowpeer(d)).start())

    def last_start():
        @pl.when(r == 1)
        def _():
            sc_fac_start(2)

    @pl.when(r == 0)
    def _():
        sc_fac_start(0)
        xs[0, 0] = rhs[:, 0:KB]
        w[0, c] = own[0, 0, 0:8]

    @pl.when(r == 1)
    def _():
        sc_fac_start(1)
        r1[...] = rhs[:, KB : 2 * KB]
        w[1, c] = own[0, 0, 8:16]
        w[2, c] = own[1, :, 1]

    def swap(q):
        return remote(own.at[q], other.at[q], s_l.at[q], r_l.at[q], mate)

    for q in range(2):
        swap(q).start()

    def convert(src, lane):
        def step(i):
            at = pl.ds(pl.multiple_of(i * 256, 256), 256)
            for q in range(2):
                hi, lo = split(src[q, i].reshape(256, KB))
                lhi[q, at, cols(lane)] = hi
                llo[q, at, cols(lane)] = lo

        loop(0, NZ, step)

    def ag(b, d):
        return remote(xs.at[b, r], xs.at[b, r], s_ag.at[b, d], r_ag.at[b, r], (rowpeer(d), c))

    def ag_in(b, d):
        p = rowpeer(d)
        return remote(xs.at[b, p], xs.at[b, p], s_ag.at[b, d], r_ag.at[b, p], (p, c))

    def ag_start(b):
        loop(1, NR, lambda d: ag(b, d).start())

    def ag_wait(b):
        loop(1, NR, lambda d: ag_in(b, d).wait_recv())

    def zcopy(q, h, i, far_z, d):
        k = 2 * far_z + core
        return remote(half(q, k, h), half(q, k, h), s_z.at[q, h, i], r_z.at[q, h, far_z], (r, 2 * zpeer(d) + core))

    def zfirst(q, h):
        return [zcopy(q, h, i, z, d) for i, d in enumerate((2, NZ - 2, 1, NZ - 1))]

    def zsecond(q, h):
        left, right = zpeer(NZ - 2), zpeer(2)
        last = zcopy(q, h, 6, left, 2) if h == 0 else zcopy(q, h, 6, right, NZ - 2)
        return [last, zcopy(q, h, 4, left, 1), zcopy(q, h, 5, right, NZ - 1)]

    def zin(q, h, d):
        zcopy(q, h, 0, zpeer(d), 1).wait_recv()

    def xsend(q, d):
        k = 2 * zpeer(d) + core
        return remote(w.at[q, k], w.at[q, k], s_cx.at[q, d], r_cx.at[q, zpeer(d)], mate)

    def xrecv(q, d):
        k = 2 * zpeer(d) + 1 - core
        return remote(w.at[q, k], w.at[q, k], s_cx.at[q, d], r_cx.at[q, zpeer(d)], mate)

    def ready(q, k):
        hi, lo = split(w[q, k].reshape(KB, KB))
        at = cols(k)
        wb[q, 0:KB, at] = hi
        wb[q, KB : 2 * KB, at] = lo

    def slice_in(q, h):
        @pl.when(r != source(q))
        def _():
            remote(half(q, c, h), half(q, c, h), s_rhs.at[0], r_sc.at[q, h], (rowpeer(1), c)).wait_recv()

    def fetch(q):
        for h in range(2):
            relay_go(q, h)
            slice_in(q, h)
            for cp in zfirst(q, h):
                cp.start()
        xsend(q, 0).start()
        ready(q, c)

    def hand_on(q, h):
        zin(q, h, 2)
        zin(q, h, NZ - 2)
        for cp in zsecond(q, h):
            cp.start()

    def near(q):
        for d in (2, NZ - 2):
            xsend(q, d).start()
            ready(q, 2 * zpeer(d) + core)
        arrive(q, (1, NZ - 1))

    def arrive(q, which):
        for d in which:
            for h in range(2):
                zin(q, h, d)
            xsend(q, d).start()
            ready(q, 2 * zpeer(d) + core)

    def collect(q):
        def step(d):
            xrecv(q, d).wait_recv()
            ready(q, 2 * zpeer(d) + 1 - core)

        loop(0, NZ, step)

    def load_x(b):
        def step(k):
            hi, lo = split(xs[b, k])
            xb[0:MB, cols(k)] = hi
            xb[MB : 2 * MB, cols(k)] = lo

        loop(0, NR, step)

    def product(q):
        o = dot_nt(xb[...], wb[q])
        return o[0:MB, 0:KB] + o[MB : 2 * MB, 0:KB] + o[0:MB, KB : 2 * KB]

    def rhs0_in():
        @pl.when(r != 0)
        def _():
            remote(xs.at[0, r], xs.at[0, r], s_rhs.at[0], r_rhs.at[0], (rowpeer(1), c)).wait_recv()

    def rhs1_in():
        @pl.when(r != 1)
        def _():
            remote(r1, r1, s_rhs.at[0], r_rhs.at[1], (rowpeer(1), c)).wait_recv()

    def swap_in():
        for q in range(2):
            swap(q).wait_recv()

    def zorder(i):
        h = (i + 1) // 2
        return h + (i + 1) % 2 * (NZ - 2 * h)

    def a2a(d):
        p = zpeer(d)
        return remote(xs.at[1, pl.ds(2 * p, 2)], t.at[z], s_a.at[0, d], r_a.at[0, z], (r, 2 * p + core))

    def a2a_from(p):
        d = 1
        return remote(t.at[p], t.at[p], s_a.at[0, d], r_a.at[0, p], (r, 2 * p + core))

    def regroup(d):
        p = zpeer(d)
        return remote(py.at[p], pz.at[z], s_a.at[1, d], r_a.at[1, z], (r, 2 * p + core))

    def regroup_in(d):
        p = zpeer(d)
        return remote(pz.at[p], pz.at[p], s_a.at[1, d], r_a.at[1, p], (r, 2 * p + core))

    def spread(g, d):
        return remote(gx.at[g, r], gx.at[g, r], s_g.at[g, d], r_g.at[g, r], (rowpeer(d), c))

    def spread_in(g, d):
        p = rowpeer(d)
        return remote(gx.at[g, p], gx.at[g, p], s_g.at[g, d], r_g.at[g, p], (p, c))

    def to_owner():
        return remote(py, s1t.at[:, r], s_o, r_o.at[r], (1, c))

    def from_peer(d):
        p = rowpeer(d)
        return remote(py, s1t.at[:, p], s_o, r_o.at[p], (p, c))

    def dest(way, s):
        return (z + NZ - 1 - s) % NZ if way == 0 else (z + 1 + s) % NZ

    def hop(way, s, j):
        lanes = pl.ds(way * HALF + j * PIECE, PIECE)
        to = (z + 1) % NZ if way == 0 else (z + NZ - 1) % NZ
        return remote(
            acc.at[dest(way, s), :, lanes], slots.at[way, s, j], s_rs.at[way, s, j], r_rs.at[way, s, j],
            (r, 2 * to + core),
        )

    def left_scatter():
        @pl.when(r == 0)
        def _():
            loop(1, NR, lambda d: sc_rhs(0, rowpeer(d)).wait_send())
            sc_fac_left(0)

        @pl.when(r == 1)
        def _():
            loop(1, NR, lambda d: sc_rhs(1, rowpeer(d)).wait_send())
            sc_fac_left(1)
            sc_fac_left(2)

        for which in range(3):

            @pl.when(is_relay(which))
            def _(which=which):
                for h in range(2):
                    relay(which, h).wait_send()

    def left_swap():
        for q in range(2):
            swap(q).wait_send()

    def left_f(q):
        for h in range(2):
            for cp in zfirst(q, h) + zsecond(q, h):
                cp.wait_send()
        loop(0, NZ, lambda d: xsend(q, d).wait_send())

    def left_ag(b):
        loop(1, NR, lambda d: ag(b, d).wait_send())

    def left_a2a():
        loop(1, NZ, lambda d: a2a(d).wait_send())

    def left_regroup():
        loop(1, NZ, lambda d: regroup(d).wait_send())

    def left_spread():
        loop(1, NR, lambda d: spread(1, d).wait_send())

    def drain(s):
        for way in range(2):
            for j in range(SUB):
                hop(way, s, j).wait_send()

    convert(own, core)
    fetch(0)
    rhs_start(0)
    fetch(1)
    last_start()
    rhs_start(1)
    hand_on(0, 0)
    hand_on(0, 1)
    rhs0_in()
    ag_start(0)
    near(0)
    hand_on(1, 0)
    hand_on(1, 1)
    arrive(0, (3, NZ - 3, 4))
    near(1)
    fetch(2)
    ag_wait(0)
    load_x(0)
    collect(0)
    xs[1, r] = product(0)
    ag_start(1)
    hand_on(2, 0)
    hand_on(2, 1)
    arrive(1, (3, NZ - 3, 4))
    near(2)
    arrive(2, (3, NZ - 3, 4))
    ag_wait(1)
    load_x(1)
    collect(1)
    rhs1_in()
    xs[2, r] = r1[...] - product(1)
    ag_start(2)
    loop(1, NZ, lambda d: a2a(d).start())
    t[z] = xs[1, pl.ds(2 * z, 2)]
    swap_in()
    convert(other, 1 - core)
    left_swap()
    for q in range(2):
        left_f(q)
        left_ag(q)
    ag_wait(2)
    collect(2)
    load_x(2)
    turned = dot_nt(wb[2], xb[0:MB, :])
    turned = turned[0:KB] + turned[KB : 2 * KB] + dot_nt(wb[2, 0:KB, :], xb[MB : 2 * MB, :])
    py[:, :, 0:MB] = turned.reshape(NZ, 16, MB)
    loop(1, NZ, lambda d: regroup(d).start())
    pz[z] = py[z]

    left_f(2)
    left_ag(2)
    loop(1, NZ, lambda d: regroup_in(d).wait_recv())

    def pair(g):
        return (z + NZ - 1 - g) % NZ, z if g == 3 else (z + 1 + g) % NZ

    def spread_start(g):
        for i in range(2):
            one, two = pair(2 * g + i)
            gx[g, r, i] = pz[one] + pltpu.roll(pz[two], MB, 1)
        loop(1, NR, lambda d: spread(g, d).start())

    def spread_end(g):
        loop(1, NR, lambda d: spread_in(g, d).wait_recv())
        for n in range(2):
            for k in range(2):
                hi, lo = split(gx[g, 8 * k : 8 * k + 8, n].reshape(KB, KB).T)
                for i, d in enumerate(pair(2 * g + n)):
                    rows = pl.ds(pl.multiple_of(d * MB, MB), MB)
                    tb[0, rows, k * KB : (k + 1) * KB] = hi[i * MB : (i + 1) * MB]
                    tb[1, rows, k * KB : (k + 1) * KB] = lo[i * MB : (i + 1) * MB]

    spread_start(0)

    def first_in(d, away):
        if away:
            a2a_from(d).wait_recv()
        rows = pl.ds(pl.multiple_of(d * MB, MB), MB)
        for k in range(2):
            hi, lo = split(t[d, k])
            ta[0, rows, k * KB : (k + 1) * KB] = hi
            ta[1, rows, k * KB : (k + 1) * KB] = lo

    def first_in_step(s):
        first_in(dest(0, s), True)
        first_in(z if s == 3 else dest(1, s), s != 3)

    def part(q, way, s):
        d = dest(way, s)
        rows = pl.ds(pl.multiple_of(d * MB, MB), MB)
        from_ = ta if q == 0 else tb
        hi, lo = from_[0, rows, :], from_[1, rows, :]
        for j in range(HALF // 512):
            at = slice(way * HALF + j * 512, way * HALF + (j + 1) * 512)
            o = dot_nt(jnp.concatenate([hi, lo], axis=0), lhi[q, at, :])
            o = o[0:MB] + o[MB : 2 * MB] + dot_nt(hi, llo[q, at, :])
            if q == 0:
                acc[d, :, at] = o
            else:
                acc[d, :, at] += o

    def parts(q, s):
        for way in range(2):
            part(q, way, s)

    def pass_on(way, s, j):
        if not (isinstance(s, int) and s == NZ - 1):
            hop(way, s, j).start()

    def ring(s):
        if isinstance(s, int) and s == 1:
            spread_end(1)
            parts(1, 2)
        for j in range(SUB):
            for way in range(2):
                lanes = slice(way * HALF + j * PIECE, way * HALF + (j + 1) * PIECE)
                hop(way, s, j).wait_recv()
                acc[dest(way, s + 1), :, lanes] += slots[way, s, j]
                pass_on(way, s + 1, j)
            if j == 1 and not (isinstance(s, int) and s == 0):
                drain(s - 1)
            if isinstance(s, int) and s == 6:
                continue
            if j == 0 and isinstance(s, int) and s < 2:
                first_in_step(s + 2)
            if j < 2:
                part(0, j, s + 2)
            elif not (isinstance(s, int) and s == 0):
                part(1, j - 2, s + 2)

    for s in range(2):
        first_in_step(s)
        parts(0, s)
    loop(1, NR, lambda d: spread(0, d).wait_send())
    spread_start(1)
    spread_end(0)

    def left_late():
        left_a2a()
        left_regroup()
        left_spread()

    @pl.when(r > 1)
    def _():
        for way in range(2):
            part(1, way, 0)
            for j in range(SUB):
                hop(way, 0, j).start()
        parts(1, 1)
        left_late()
        ring(0)
        ring(1)
        to_owner().start()
        loop(2, NZ - 2, ring)
        ring(NZ - 2)
        out_ref[...] = rhs[...] - acc[z]
        to_owner().wait_send()
        drain(NZ - 2)

    def no_ring():
        spread_end(1)
        first_in_step(2)
        first_in_step(3)
        left_late()

    @pl.when(r == 0)
    def _():
        no_ring()
        to_owner().start()
        for k in range(NR):
            out_ref[:, k * KB : (k + 1) * KB] = xs[1, k]
        to_owner().wait_send()

    @pl.when(r == 1)
    def _():
        no_ring()
        s1t[:, 1] = py[...]
        loop(1, NR, lambda d: from_peer(d).wait_recv())
        for k in range(NR):
            block = s1t[k // 2, k % 2 * 8 : k % 2 * 8 + 8].reshape(KB, KB)
            out_ref[:, k * KB : (k + 1) * KB] = block.T[0:MB]

    left_scatter()


def local(right_side, factor):
    rows = factor.shape[0]
    dma = pltpu.SemaphoreType.DMA
    return pl.pallas_call(
        kernel,
        name="panels",
        out_shape=jax.ShapeDtypeStruct((MB, NB), F32),
        in_specs=[pl.BlockSpec(memory_space=pl.ANY)] * 2,
        out_specs=pl.BlockSpec(memory_space=pltpu.VMEM),
        scratch_shapes=[
            pltpu.VMEM((2 * NB, KB), F32),
            pltpu.VMEM((MB, NB), F32),
            pltpu.VMEM((2, NZ, 16, 16, KB), F32),
            pltpu.VMEM((2, NZ, 16, 16, KB), F32),
            pltpu.VMEM((2, NB, 2 * KB), BF16),
            pltpu.VMEM((2, NB, 2 * KB), BF16),
            pltpu.VMEM((3, 16, 8, 16, KB), F32),
            pltpu.VMEM((3, 8, 16, KB), F32),
            pltpu.VMEM((3, 2 * KB, NB), BF16),
            pltpu.VMEM((3, NR, MB, KB), F32),
            pltpu.VMEM((MB, KB), F32),
            pltpu.VMEM((2 * MB, NB), BF16),
            pltpu.VMEM((NZ, 2, MB, KB), F32),
            pltpu.VMEM((NZ, 16, KB), F32),
            pltpu.VMEM((NZ, 16, KB), F32),
            pltpu.VMEM((2, NR, 2, 16, KB), F32),
            pltpu.VMEM((NZ, NR, 16, KB), F32),
            pltpu.VMEM((2, MC, 2 * KB), BF16),
            pltpu.VMEM((2, MC, 2 * KB), BF16),
            pltpu.VMEM((NZ, MB, NB), F32),
            pltpu.VMEM((2, NZ - 1, SUB, MB, PIECE), F32),
            dma((2,)),
            dma((NR,)),
            dma((2,)),
            dma((3, 2, NR)),
            dma((3, 2)),
            dma((3, 2)),
            dma((3, 2)),
            dma((3, 2, 7)),
            dma((3, 2, NZ)),
            dma((3, NZ)),
            dma((3, NZ)),
            dma((3, NR)),
            dma((3, NR)),
            dma((2, NZ)),
            dma((2, NZ)),
            dma((2, NR)),
            dma((2, NR)),
            dma,
            dma((NR,)),
            dma((2,)),
            dma((2,)),
            dma((2, NZ - 1, SUB)),
            dma((2, NZ - 1, SUB)),
        ],
        compiler_params=pltpu.CompilerParams(
            collective_id=0, has_side_effects=True, vmem_limit_bytes=60 * 2**20
        ),
    )(right_side, factor.reshape(2 * rows, KB))


def solution(mesh):
    in_specs = (P("col", "row"), P("row", None, "col"))
    out_specs = P("col", "row")
    return jax.shard_map(local, mesh=mesh, in_specs=in_specs, out_specs=out_specs, check_vma=False)
```
